128 devices in a mesh: row: 8 (over y, core), col: 16 (over x, z).
Axes of the slice: x: 4, y: 4, z: 4, core: 2. Of those that a mesh axis runs over, the one named last changes fastest.
Arguments:
- tokens: bfloat16 [1024, 16384], P('col', 'row'), may hold values from -6 to 6
- segment_ids: int32 [1024], replicated, may hold values from 0 to 3, never falling along the last dimension, each value on 1 to 512 neighbouring positions
- w_query: bfloat16 [16384, 16384], P('row', 'col'), may hold values from -8 to 8
- w_key: bfloat16 [16384, 1024], P('row', 'col'), may hold values from -8 to 8
- value_weight: bfloat16 [16384, 1024], P('row', 'col'), may hold values from -0.046875 to 0.046875
- w_out: bfloat16 [16384, 16384], P('col', 'row'), may hold values from -0.046875 to 0.046875
- grad_out: bfloat16 [1024, 16384], P('col', 'row'), may hold values from -6 to 6
Outputs:
- mixed: bfloat16 [1024, 16384], P('col', 'row')
- grad_tokens: bfloat16 [1024, 16384], P('col', 'row')
- grad_w_query: bfloat16 [16384, 16384], P('row', 'col')
- grad_w_key: bfloat16 [16384, 1024], P('row', 'col')
- grad_w_value: bfloat16 [16384, 1024], P('row', 'col')
- grad_w_out: bfloat16 [16384, 16384], P('col', 'row')
The draws below stay inside these ranges and needn't reach their ends.
Inputs may be any that keep to these rules, and one draw needn't show every extreme that they name: `segment_ids`: document ids never fall along the tokens; each document holds 1 to 512 tokens, and one holds exactly 512.
All inputs are finite; a program needn't handle non-finite values.
Results may differ from the reference program's by a relative error of at most 0.04.
The reference program's roundings to bfloat16 on the way count: a program that leaves them out, or rounds other values in their place, can miss the bound.
Values may be sent and summed in bfloat16 or wider, within the bound.
A program may use at most 128 MiB of HBM per device.

```python
import math
import jax
import jax.numpy as jnp
import numpy as np
from jax import lax

MODEL_WIDTH = 16384
QUERY_HEADS = 128
KEY_VALUE_HEADS = 8
HEAD_SIZE = 128
TOKENS = 1024


def draw_w_key(key, part):
    key = jax.random.fold_in(key, 5)
    weight_tensors = jax.random.truncated_normal(key, -6.0, 6.0, (MODEL_WIDTH, KEY_VALUE_HEADS * HEAD_SIZE), jnp.float32) * MODEL_WIDTH ** (-0.5)
    return weight_tensors.astype(jnp.bfloat16)


def draw_w_query(key, part):
    key = jax.random.fold_in(key, 6)
    weight_tensors = jax.random.truncated_normal(jax.random.fold_in(key, 1), -6.0, 6.0, (MODEL_WIDTH, QUERY_HEADS * HEAD_SIZE), jnp.float32) * MODEL_WIDTH ** (-0.5)
    return weight_tensors.astype(jnp.bfloat16)


def block_levels(own_key, dims, cuts, least, high):
    level, own = 1.0, jax.random.fold_in(own_key, 6)
    for axis_at, blocks in cuts:
        heights = jnp.exp(jax.random.uniform(jax.random.fold_in(own, axis_at), (blocks,), jnp.float32, least / len(cuts), high / len(cuts)))
        level = level * jnp.repeat(heights, dims[axis_at] // blocks).reshape([-1 if axis == axis_at else 1 for axis in range(len(dims))])
    return level


def length_profile(count, total, most, skew):
    weights = [(1 << 20) // math.isqrt(rank ** skew) + 1 for rank in range(2, count + 1)]
    rest, counts = total - most - (count - 1), [1] * (count - 1)
    while rest > 0:
        free = [i for i in range(count - 1) if counts[i] < most]
        whole, budget = sum([weights[i] for i in free]), rest
        for i in free:
            more = min(most - counts[i], max(1, budget * weights[i] // whole), rest)
            counts[i] = counts[i] + more
            rest = rest - more
    return np.array([most] + counts)


def uneven_parts(stream_key, count, total, most, skew):
    if count == 2:
        one = jax.random.randint(stream_key, (), max(1, total - most), min(most, total - 1) + 1)
        return jnp.stack([one, total - one])
    lengths = jnp.asarray(length_profile(count, total, most, skew), jnp.int32)
    pairs = (count - 1) // 2
    donor, receiver = lengths[1:1 + 2 * pairs:2], lengths[2:2 + 2 * pairs:2]
    room = jnp.minimum(donor - 1, most - receiver)
    moved = jax.random.randint(jax.random.fold_in(stream_key, 1), (pairs,), 0, 1 << 20) % (room + 1)
    lengths = lengths.at[1:1 + 2 * pairs:2].set(donor - moved).at[2:2 + 2 * pairs:2].set(receiver + moved)
    return lengths[jax.random.permutation(jax.random.fold_in(stream_key, 2), count)]


def bell_draw(rng, dims, spread, most, pieces=(), held_as=jnp.bfloat16):
    loudness = block_levels(rng, dims, pieces, -0.22, 0.18) if pieces else 1.0
    entries = jax.random.normal(rng, dims, jnp.float32) * spread * loudness
    return jnp.minimum(jnp.maximum(entries, -most), most).astype(held_as)


def setup_inputs(seed: int = 0) -> dict:
    arg_keys = jax.random.split(jax.random.key(seed), 8)
    return {
        "tokens": bell_draw(arg_keys[0], (TOKENS, MODEL_WIDTH), 1.0, 6.0, ((0, 16), (1, 8))),
        "segment_ids": jnp.searchsorted(jnp.cumsum(uneven_parts(arg_keys[1], 4, TOKENS, TOKENS // 2, 0)), jnp.arange(TOKENS), side="right").astype(jnp.int32),
        "w_query": draw_w_query(jax.random.fold_in(arg_keys[7], 71), 0),
        "w_key": draw_w_key(jax.random.fold_in(arg_keys[7], 71), 0),
        "value_weight": bell_draw(arg_keys[4], (MODEL_WIDTH, KEY_VALUE_HEADS * HEAD_SIZE), MODEL_WIDTH ** -0.5, 0.046875, ((0, 8), (1, 16))),
        "w_out": bell_draw(arg_keys[5], (QUERY_HEADS * HEAD_SIZE, MODEL_WIDTH), (QUERY_HEADS * HEAD_SIZE) ** -0.5, 0.046875, ((0, 16), (1, 8))),
        "grad_out": bell_draw(arg_keys[6], (TOKENS, MODEL_WIDTH), 1.0, 6.0, ((0, 16), (1, 8))),
    }


def attention_probs(query_matrix, keys_block, allowed, scale):
    scores = jnp.einsum("rgd,sd->grs", query_matrix.astype(jnp.float32), keys_block.astype(jnp.float32)) * scale
    scores = jnp.where(allowed[None] > 0, scores, jnp.float32(-1e30))
    highest = jnp.max(scores, axis=-1, keepdims=True)
    expo = jnp.exp(scores - highest)
    return expo / jnp.sum(expo, axis=-1, keepdims=True)


def forward_group(query_matrix, keys_block, values_block, allowed, scale):
    probs = attention_probs(query_matrix, keys_block, allowed, scale)
    probs_low = probs.astype(jnp.bfloat16)
    result = jnp.einsum("grs,sd->rgd", probs_low.astype(jnp.float32), values_block.astype(jnp.float32))
    return result.astype(jnp.bfloat16)


def backward_group(query_matrix, keys_block, values_block, grad_heads, allowed, scale):
    probs = attention_probs(query_matrix, keys_block, allowed, scale)
    probs_low = probs.astype(jnp.bfloat16)
    grad_probs = jnp.einsum("rgd,sd->grs", grad_heads.astype(jnp.float32), values_block.astype(jnp.float32))
    inner = jnp.sum(probs * grad_probs, axis=-1, keepdims=True)
    grad_scores = (probs * (grad_probs - inner) * scale).astype(jnp.bfloat16)
    grad_q = jnp.einsum("grs,sd->rgd", grad_scores.astype(jnp.float32), keys_block.astype(jnp.float32)).astype(jnp.bfloat16)
    key_gradient_rows = jnp.einsum("grs,rgd->sd", grad_scores.astype(jnp.float32), query_matrix.astype(jnp.float32))
    value_gradient_rows = jnp.einsum("grs,rgd->sd", probs_low.astype(jnp.float32), grad_heads.astype(jnp.float32))
    return grad_q, key_gradient_rows, value_gradient_rows


def contract_last(left, right):
    return lax.dot_general(left, right, (((1,), (1,)), ((), ())), preferred_element_type=jnp.float32)


def contract_first(left, right):
    return lax.dot_general(left, right, (((0,), (0,)), ((), ())), preferred_element_type=jnp.float32)


def reference(tokens, segment_ids, w_query, w_key, value_weight, w_out, grad_out):
    sequence_length = tokens.shape[0]
    head_group = QUERY_HEADS // KEY_VALUE_HEADS
    scale = HEAD_SIZE ** -0.5
    query_matrix = jnp.dot(tokens, w_query, preferred_element_type=jnp.float32).astype(jnp.bfloat16)
    every_key = jnp.dot(tokens, w_key, preferred_element_type=jnp.float32).astype(jnp.bfloat16)
    every_value = jnp.dot(tokens, value_weight, preferred_element_type=jnp.float32).astype(jnp.bfloat16)
    positions = jnp.arange(sequence_length, dtype=jnp.int32)
    allowed = ((segment_ids[:, None] == segment_ids[None, :]) & (positions[None, :] <= positions[:, None])).astype(jnp.int32)
    grouped_queries = query_matrix.reshape(sequence_length, KEY_VALUE_HEADS, head_group, HEAD_SIZE).transpose(1, 0, 2, 3)
    grouped_keys = every_key.reshape(sequence_length, KEY_VALUE_HEADS, HEAD_SIZE).transpose(1, 0, 2)
    grouped_values = every_value.reshape(sequence_length, KEY_VALUE_HEADS, HEAD_SIZE).transpose(1, 0, 2)
    outputs = lax.map(lambda members: forward_group(members[0], members[1], members[2], allowed, scale), (grouped_queries, grouped_keys, grouped_values))
    attended = outputs.transpose(1, 0, 2, 3).reshape(sequence_length, QUERY_HEADS * HEAD_SIZE)
    mixed = jnp.dot(attended, w_out, preferred_element_type=jnp.float32).astype(jnp.bfloat16)
    attended_gradient = contract_last(grad_out, w_out).astype(jnp.bfloat16)
    grad_w_out = contract_first(attended, grad_out).astype(jnp.bfloat16)
    group_gradients = attended_gradient.reshape(sequence_length, KEY_VALUE_HEADS, head_group, HEAD_SIZE).transpose(1, 0, 2, 3)
    grad_q, key_gradient_rows, value_gradient_rows = lax.map(lambda members: backward_group(members[0], members[1], members[2], members[3], allowed, scale), (grouped_queries, grouped_keys, grouped_values, group_gradients))
    grad_query = grad_q.transpose(1, 0, 2, 3).reshape(sequence_length, QUERY_HEADS * HEAD_SIZE)
    key_gradient = key_gradient_rows.transpose(1, 0, 2).reshape(sequence_length, KEY_VALUE_HEADS * HEAD_SIZE).astype(jnp.bfloat16)
    value_gradient = value_gradient_rows.transpose(1, 0, 2).reshape(sequence_length, KEY_VALUE_HEADS * HEAD_SIZE).astype(jnp.bfloat16)
    grad_tokens = (contract_last(grad_query, w_query) + contract_last(key_gradient, w_key) + contract_last(value_gradient, value_weight)).astype(jnp.bfloat16)
    grad_w_query = contract_first(tokens, grad_query).astype(jnp.bfloat16)
    grad_w_key = contract_first(tokens, key_gradient).astype(jnp.bfloat16)
    grad_w_value = contract_first(tokens, value_gradient).astype(jnp.bfloat16)
    return mixed, grad_tokens, grad_w_query, grad_w_key, grad_w_value, grad_w_out
```

```python
import jax
import jax.numpy as jnp
from jax import lax
from jax.experimental import pallas as pl
from jax.experimental.pallas import tpu as pltpu
from jax.sharding import PartitionSpec as P

HEAD = 128
CHUNKS = 8
TILE = 256
MESH = pl.DeviceIdType.MESH
F32 = jnp.float32
BF16 = jnp.bfloat16


def nn(left, right):
    return jnp.dot(left, right, preferred_element_type=F32)


def nt(left, right):
    return lax.dot_general(left, right, (((1,), (1,)), ((), ())), preferred_element_type=F32)


def tn(left, right):
    return lax.dot_general(left, right, (((0,), (0,)), ((), ())), preferred_element_type=F32)


def ring(value, step):
    return lax.rem(value + (step + 4), 4)


class Copies:
    def __init__(self, send, recv):
        self.send, self.recv = send, recv
        self.made = {}
        self.sent = set()

    def start(self, key, src, dst, device):
        index = len(self.made)
        copy = pltpu.make_async_remote_copy(
            src_ref=src,
            dst_ref=dst,
            send_sem=self.send.at[index],
            recv_sem=self.recv.at[index],
            device_id=device,
            device_id_type=MESH,
        )
        copy.start()
        self.made[key] = copy

    def arrived(self, *keys):
        for key in keys:
            self.made[key].wait_recv()

    def left(self, *keys):
        for key in keys:
            if key not in self.sent:
                self.made[key].wait_send()
                self.sent.add(key)

    def finish(self):
        self.left(*list(self.made))


SEMS = 160
VMEM_LIMIT = 64 * 2**20


def kernel(
    tokens, grad_out, wq_in, wk_in, wv_in, wo_in, mrow, mcol,
    mixed, gtokens, gwq, gwk, gwv, gwo,
    tok, grd, wq, wk, wv, wkv, wo,
    pt, xt, r1t, r2t, pg, xg, r1g, r2g, pd, xd, r1d, r2d,
    qr, kvp, kvo, gh, kv, mask, probs, dkt, dvt, dsum, dout, dback,
    att, gq, gkv,
    stfar, stnear, own, f1, f2, n1, n2, pfar, pnear, outst,
    send, recv, local, out_sem,
):
    row, col = lax.axis_index("row"), lax.axis_index("col")
    y, core = row // 2, lax.rem(row, 2)
    x, z = col // 4, lax.rem(col, 4)
    width = tok.shape[-1]
    heads = qr.shape[-1] // HEAD
    hn = heads * HEAD
    scale = HEAD ** (-0.5)

    def at_x(step):
        return {"col": ring(x, step) * 4 + z}

    def at_z(step):
        return {"col": x * 4 + ring(z, step)}

    def at_y(step):
        return {"row": ring(y, step) * 2 + core}

    at_core = {"row": y * 2 + (1 - core)}
    odd = lax.rem(z, 2)
    at_partner = {"col": x * 4 + (z + 1 - 2 * odd)}

    loads = [
        pltpu.make_async_copy(wq_in, wq, local.at[0]),
        pltpu.make_async_copy(wk_in, wk, local.at[1]),
        pltpu.make_async_copy(wv_in, wv, local.at[2]),
        pltpu.make_async_copy(wo_in, wo, local.at[3]),
    ]
    half = 32
    own_copies = []
    for n, (src, buf) in enumerate(((tokens, tok), (grad_out, grd))):
        own_copies.append(
            [
                pltpu.make_async_copy(src.at[0:half], buf.at[0, z, x], local.at[4 + 2 * n]),
                pltpu.make_async_copy(src.at[half:], buf.at[1, x, z], local.at[5 + 2 * n]),
            ]
        )
    for pair in own_copies:
        for copy in pair:
            copy.start()
    for copy in loads:
        copy.start()

    barrier = pltpu.get_barrier_semaphore()
    for device in (at_x(1), at_x(-1), at_z(1), at_z(-1), at_y(1), at_y(-1), at_core):
        pl.semaphore_signal(barrier, inc=1, device_id=device, device_id_type=MESH)
    pl.semaphore_wait(barrier, 7)

    cp = Copies(send, recv)

    def axes(h):
        return ((at_x, x), (at_z, z)) if h == 0 else ((at_z, z), (at_x, x))

    def ag1(name, src, buf):
        for h in range(2):
            (first, f), (_, s) = axes(h)
            for d in (1, -1):
                cp.start((name, 1, h, d), src.at[h * half : (h + 1) * half], buf.at[h, s, f], first(d))

    def ag1b(name, buf):
        for h in range(2):
            (first, f), (_, s) = axes(h)
            cp.arrived((name, 1, h, 1), (name, 1, h, -1))
            for d, lo in ((1, 0), (-1, 16)):
                part = buf.at[h, s, ring(f, -d), lo : lo + 16]
                cp.start((name, 2, h, d), part, part, first(d))

    def ag2(name, buf):
        for h in range(2):
            _, (second, s) = axes(h)
            cp.arrived((name, 2, h, 1), (name, 2, h, -1))
            for d in (1, -1):
                cp.start((name, 3, h, d), buf.at[h, s], buf.at[h, s], second(d))

    def ag2b(name, buf):
        for h in range(2):
            _, (second, s) = axes(h)
            cp.arrived((name, 3, h, 1), (name, 3, h, -1))
            for d, lo in ((1, 0), (-1, 2)):
                part = buf.at[h, ring(s, -d), lo : lo + 2]
                cp.start((name, 4, h, d), part, part, second(d))

    def ag_end(name):
        for h in range(2):
            cp.arrived((name, 4, h, 1), (name, 4, h, -1))

    steps = (0, 1, -1, 2)
    pairs = [(ring(z, s), ring(x, s)) for s in steps]

    def load_pair(buf, p):
        bz, bx = pairs[p]
        return jnp.concatenate(
            [buf[0, bz].reshape(128, width), buf[1, bx].reshape(128, width)], axis=0
        )

    def put_partial(dst, p, value, columns):
        size = value.shape[-1]
        five = value.reshape(2, 2, 4, 16, size)
        for h in range(2):
            for c in range(2):
                dst[c, 2 * p + h, :, :, columns] = five[h, c]

    def project(p):
        def body(n, carry):
            cols = pl.ds(pl.multiple_of(n * TILE, TILE), TILE)
            put_partial(pt, p, nn(load_pair(tok, p), wq[:, cols]), cols)
            return carry

        lax.fori_loop(0, hn // TILE, body, 0)
        put_partial(pt, p, nn(load_pair(tok, p), wkv[...]), pl.ds(hn, 128))

    def project_grad(p):
        def body(n, carry):
            cols = pl.ds(pl.multiple_of(n * TILE, TILE), TILE)
            put_partial(pg, p, nt(load_pair(grd, p), wo[cols, :]), cols)
            return carry

        lax.fori_loop(0, hn // TILE, body, 0)

    def rs_core(name, part, held, s0, n):
        cp.start(
            (name, "c", s0), part.at[1 - core, pl.ds(s0, n)], held.at[pl.ds(s0, n)], at_core
        )

    def rs_y1(name, part, held, r1, s0, n):
        cp.arrived((name, "c", s0))
        for s in range(s0, s0 + n):
            held[s] = held[s] + part[core, s]
        for i, d in enumerate((1, -1)):
            cp.start(
                (name, "y1", s0, d),
                held.at[pl.ds(s0, n), ring(y, 2), 8 * i : 8 * i + 8],
                r1.at[i, pl.ds(s0, n)],
                at_y(d),
            )

    def rs_y2(name, held, r1, r2, s0, n):
        cp.arrived((name, "y1", s0, 1), (name, "y1", s0, -1))
        for i, d in enumerate((1, -1)):
            t = ring(y, d)
            lo = 8 * i
            for s in range(s0, s0 + n):
                held[s, t, lo : lo + 8] = held[s, t, lo : lo + 8] + r1[i, s]
            cp.start(
                (name, "y2", s0, d), held.at[pl.ds(s0, n), t], r2.at[i, pl.ds(s0, n)], at_y(d)
            )

    def rs_wait(name, s0):
        cp.arrived((name, "y2", s0, 1), (name, "y2", s0, -1))

    def rs_value(held, r2, s):
        return held[s, y] + r2[0, s] + r2[1, s]

    def chunk_of(slot):
        bz, bx = pairs[slot // 2]
        return bz if slot % 2 == 0 else 4 + bx

    def fin_tokens(s0, n):
        rs_wait("t", s0)
        for s in range(s0, s0 + n):
            total = rs_value(xt, r2t, s).astype(BF16)
            qr[chunk_of(s)] = total[:, :hn]
            kvp[chunk_of(s)] = total[:, hn:]

    def fin_grads(s0, n):
        rs_wait("g", s0)
        for s in range(s0, s0 + n):
            gh[chunk_of(s)] = rs_value(xg, r2g, s).astype(BF16)

    def agr1(name, buf):
        mine = buf.at[:, core, y]
        for d in (1, -1):
            cp.start((name, "a", d), mine, mine, at_y(d))
        cp.start((name, "b", 0), mine, mine, at_core)

    def agr2(name, buf):
        cp.arrived((name, "a", 1), (name, "a", -1))
        for d, lo in ((1, 0), (-1, 4)):
            part = buf.at[lo : lo + 4, core, ring(y, -d)]
            cp.start((name, "c", d), part, part, at_y(d))
        for d in (1, -1):
            part = buf.at[:, core, ring(y, -d)]
            cp.start((name, "b", d), part, part, at_core)

    def agr3(name, buf):
        cp.arrived((name, "c", 1), (name, "c", -1))
        part = buf.at[:, core, ring(y, 2)]
        cp.start((name, "b", 2), part, part, at_core)

    def agr_end(name):
        cp.arrived(*[(name, "b", k) for k in (0, 1, -1, 2)])

    def rsc_far(name, make, w1):
        def put(k, cols, v):
            stfar[k // 2, pl.ds(2 * (k % 2), 2), :, cols] = v.astype(BF16)

        make(
            [(0, pairs[3][0], 0), (0, pairs[3][0], 1), (1, pairs[3][1], 0), (1, pairs[3][1], 1)],
            put,
        )
        for h in range(2):
            _, (second, _) = axes(h)
            for i, d in enumerate((1, -1)):
                cp.start((name, "f", h, d), stfar.at[h, 2 * i : 2 * i + 2], w1.at[h, i], second(d))

    def near_list(dep):
        items = []
        for h in range(2):
            for i in range(2):
                part = i if dep else 1 - i
                items.append((h, pairs[1 + i][h], part))
        return items

    def rsc_near(name, make, w1, w2, dep):
        if dep:
            for h in range(2):
                cp.arrived((name, "f", h, 1), (name, "f", h, -1))

        def put(k, cols, v):
            h, i = k // 2, k % 2
            part = i if dep else 1 - i
            if dep:
                v = v + w1[h, i, :, :, cols].astype(F32)
            stnear[h, i, pl.ds(2 * part, 2), :, cols] = v.astype(BF16)

        make(near_list(dep), put)
        for h in range(2):
            _, (second, _) = axes(h)
            for i, d in enumerate((1, -1)):
                part = i if dep else 1 - i
                cp.start(
                    (name, "n", h, d, dep),
                    stnear.at[h, i, 2 * part : 2 * part + 2],
                    w2.at[h, i, 2 * part : 2 * part + 2],
                    second(d),
                )

    def rsc_own(make):
        def put(k, cols, v):
            own[k // 2, pl.ds(2 * (k % 2), 2), :, cols] = v

        make(
            [(0, pairs[0][0], 0), (0, pairs[0][0], 1), (1, pairs[0][1], 0), (1, pairs[0][1], 1)],
            put,
        )

    def rsc_second(name, w2, v1):
        for h in range(2):
            (first, f), _ = axes(h)
            cp.arrived(*[(name, "n", h, d, dep) for d in (1, -1) for dep in (False, True)])
            for s in range(4):
                own[h, s] = own[h, s] + w2[h, 0, s].astype(F32) + w2[h, 1, s].astype(F32)
            pfar[h] = own[h, ring(f, 2)].astype(BF16)
            for i, d in enumerate((1, -1)):
                cp.start((name, "p", h, d), pfar.at[h, 16 * i : 16 * i + 16], v1.at[h, i], first(d))

    def rsc_third(name, v1, v2):
        for h in range(2):
            (first, f), _ = axes(h)
            cp.arrived((name, "p", h, 1), (name, "p", h, -1))
            for i, d in enumerate((1, -1)):
                t = ring(f, d)
                lo = 16 * i
                pnear[h, i, 16 - lo : 32 - lo] = own[h, t, 16 - lo : 32 - lo].astype(BF16)
                pnear[h, i, lo : lo + 16] = (
                    own[h, t, lo : lo + 16] + v1[h, i].astype(F32)
                ).astype(BF16)
                cp.start((name, "q", h, d), pnear.at[h, i], v2.at[h, i], first(d))

    def rsc_last(name, v2, dst, slot):
        copies = []
        for h in range(2):
            (_, f), _ = axes(h)
            cp.arrived((name, "q", h, 1), (name, "q", h, -1))
            outst[slot, h] = (
                own[h, f] + v2[h, 0].astype(F32) + v2[h, 1].astype(F32)
            ).astype(BF16)
            copy = pltpu.make_async_copy(
                outst.at[slot, h], dst.at[h * half : (h + 1) * half], out_sem.at[2 * slot + h]
            )
            copy.start()
            copies.append(copy)
        return copies

    def rsc_left(name):
        cp.left(*[(name, "f", h, d) for h in range(2) for d in (1, -1)])
        cp.left(*[(name, "n", h, d, e) for h in range(2) for d in (1, -1) for e in (False, True)])
        cp.left(*[(name, "p", h, d) for h in range(2) for d in (1, -1)])
        cp.left(*[(name, "q", h, d) for h in range(2) for d in (1, -1)])

    def rows_of(buf, items):
        return jnp.concatenate(
            [buf[4 * h + b, c].reshape(64, buf.shape[-1]) for h, b, c in items], axis=0
        )

    def make_mixed(items, put):
        def body(n, carry):
            cols = pl.ds(pl.multiple_of(n * TILE, TILE), TILE)
            v = nn(rows_of(att, items), wo[:, cols]).reshape(4, 2, 32, TILE)
            for k in range(4):
                put(k, cols, v[k])
            return carry

        lax.fori_loop(0, width // TILE, body, 0)

    def make_gtokens(items, put):
        def body(n, carry):
            cols = pl.ds(pl.multiple_of(n * TILE, TILE), TILE)
            v = nt(rows_of(gq, items), wq[cols, :]) + nt(rows_of(gkv, items), wkv[cols, :])
            v = v.reshape(4, 2, 32, TILE)
            for k in range(4):
                put(k, cols, v[k])
            return carry

        lax.fori_loop(0, width // TILE, body, 0)

    def keys():
        return kv[:, :, :, :, 0:HEAD].reshape(1024, HEAD)

    def vals():
        return kv[:, :, :, :, HEAD : 2 * HEAD].reshape(1024, HEAD)

    def attend():
        mi = mcol[...]
        mj = mrow[...]
        low = lax.shift_left(lax.shift_right_logical(mi, 10), 10)
        mask[...] = ((mj >= low) & (mj <= mi)).astype(jnp.int32)

        def body(h, carry):
            cols = pl.ds(pl.multiple_of(h * HEAD, HEAD), HEAD)
            q = qr[:, :, cols].reshape(128, HEAD)
            s = nt(q, keys()) * scale
            s = jnp.where(mask[...] > 0, s, F32(-1e30))
            e = jnp.exp(s - jnp.max(s, axis=-1, keepdims=True))
            p = e / jnp.sum(e, axis=-1, keepdims=True)
            probs[h] = p
            o = nn(p.astype(BF16), vals()).astype(BF16)
            att[:, core, y, :, cols] = o.reshape(CHUNKS, 16, HEAD)
            return carry

        lax.fori_loop(0, heads, body, 0)

    def attend_back():
        dkt[...] = jnp.zeros_like(dkt)
        dvt[...] = jnp.zeros_like(dvt)

        def body(h, carry):
            cols = pl.ds(pl.multiple_of(h * HEAD, HEAD), HEAD)
            q = qr[:, :, cols].reshape(128, HEAD)
            g = gh[:, :, cols].reshape(128, HEAD)
            p = probs[h]
            dp = nt(g, vals())
            inner = jnp.sum(p * dp, axis=-1, keepdims=True)
            ds = (p * (dp - inner) * scale).astype(BF16)
            dq = nn(ds, keys()).astype(BF16)
            gq[:, core, y, :, cols] = dq.reshape(CHUNKS, 16, HEAD)
            dkt[...] += nn(q.T, ds)
            dvt[...] += nn(g.T, p.astype(BF16))
            return carry

        lax.fori_loop(0, heads, body, 0)

    def put_dkv():
        for lo, src in ((0, dkt), (HEAD, dvt)):
            for n in range(CHUNKS):
                block = src[:, n * 128 : (n + 1) * 128].T.reshape(2, 4, 16, HEAD)
                for c in range(2):
                    pd[c, n, :, :, lo : lo + HEAD] = block[c]

    def grad_w_out():
        def body(n, carry):
            rows = pl.ds(pl.multiple_of(n * TILE, TILE), TILE)
            left = att[:, :, :, :, rows].reshape(1024, TILE)

            def inner(m, c2):
                cols = pl.ds(pl.multiple_of(m * 512, 512), 512)
                wo[rows, cols] = tn(left, grd[:, :, :, :, cols].reshape(1024, 512)).astype(BF16)
                return c2

            lax.fori_loop(0, width // 512, inner, 0)
            pltpu.make_async_copy(wo.at[rows], gwo.at[rows], out_sem.at[4 + n]).start()
            return carry

        lax.fori_loop(0, hn // TILE, body, 0)

    def grad_w_in():
        def body(n, carry):
            rows = pl.ds(pl.multiple_of(n * TILE, TILE), TILE)
            left = tok[:, :, :, :, rows].reshape(1024, TILE)

            def inner(m, c2):
                cols = pl.ds(pl.multiple_of(m * 512, 512), 512)
                wq[rows, cols] = tn(left, gq[:, :, :, :, cols].reshape(1024, 512)).astype(BF16)
                return c2

            lax.fori_loop(0, hn // 512, inner, 0)
            both = tn(left, gkv[...].reshape(1024, 128)).astype(BF16)
            wk[rows, :] = both[:, :64]
            wv[rows, :] = both[:, 64:]
            pltpu.make_async_copy(wq.at[rows], gwq.at[rows], out_sem.at[12 + n]).start()
            return carry

        lax.fori_loop(0, width // TILE, body, 0)
        pltpu.make_async_copy(wk, gwk, local.at[1]).start()
        pltpu.make_async_copy(wv, gwv, local.at[2]).start()

    ag1("t", tokens, tok)
    ag1b("t", tok)
    for copy in own_copies[0]:
        copy.wait()
    ag2("t", tok)
    ag1("g", grad_out, grd)
    for copy in loads[:3]:
        copy.wait()
    wkv[...] = jnp.concatenate([wk[...], wv[...]], axis=1)
    project(0)
    rs_core("t", pt, xt, 0, 2)
    ag1b("g", grd)
    rs_y1("t", pt, xt, r1t, 0, 2)
    ag2b("t", tok)
    for copy in own_copies[1]:
        copy.wait()
    ag2("g", grd)
    project(1)
    project(2)
    rs_core("t", pt, xt, 2, 4)
    rs_y2("t", xt, r1t, r2t, 0, 2)
    rs_y1("t", pt, xt, r1t, 2, 4)
    ag_end("t")
    project(3)
    rs_core("t", pt, xt, 6, 2)
    fin_tokens(0, 2)
    rs_y2("t", xt, r1t, r2t, 2, 4)
    rs_y1("t", pt, xt, r1t, 6, 2)
    loads[3].wait()
    project_grad(0)
    rs_core("g", pg, xg, 0, 2)
    rs_y2("t", xt, r1t, r2t, 6, 2)
    fin_tokens(2, 4)
    fin_tokens(6, 2)
    cp.start(("kv",), kvp, kvo, at_partner)
    rs_y1("g", pg, xg, r1g, 0, 2)
    ag2b("g", grd)
    cp.arrived(("kv",))
    mine, other = kvp[...].reshape(128, 128), kvo[...].reshape(128, 128)
    is_low = jnp.full((128, 128), odd, jnp.int32) == 0
    low = jnp.where(is_low, mine, other)
    high = jnp.where(is_low, other, mine)
    joined = jnp.concatenate(
        [low[:, :64], high[:, :64], low[:, 64:], high[:, 64:]], axis=1
    )
    kv[:, core, y] = joined.reshape(CHUNKS, 16, 2 * HEAD)
    agr1("k", kv)
    project_grad(1)
    agr2("k", kv)
    project_grad(2)
    agr3("k", kv)
    rs_core("g", pg, xg, 2, 4)
    rs_y2("g", xg, r1g, r2g, 0, 2)
    agr_end("k")
    rs_y1("g", pg, xg, r1g, 2, 4)
    attend()
    agr1("o", att)
    fin_grads(0, 2)
    rs_y2("g", xg, r1g, r2g, 2, 4)
    ag_end("g")
    project_grad(3)
    rs_core("g", pg, xg, 6, 2)
    agr2("o", att)
    rs_y1("g", pg, xg, r1g, 6, 2)
    agr3("o", att)
    fin_grads(2, 4)
    rs_y2("g", xg, r1g, r2g, 6, 2)
    agr_end("o")
    rsc_far("m", make_mixed, f1.at[0])
    rsc_near("m", make_mixed, f1.at[0], f2.at[0], False)
    fin_grads(6, 2)
    attend_back()
    agr1("q", gq)
    put_dkv()
    rs_core("d", pd, xd, 0, 8)
    rsc_near("m", make_mixed, f1.at[0], f2.at[0], True)
    rsc_own(make_mixed)
    rs_y1("d", pd, xd, r1d, 0, 8)
    agr2("q", gq)
    rs_y2("d", xd, r1d, r2d, 0, 8)
    grad_w_out()
    rs_wait("d", 0)
    for n in range(CHUNKS):
        dsum[n] = rs_value(xd, r2d, n)
    total = dsum[...].reshape(128, 2 * HEAD)
    lower = jnp.concatenate([total[:, 0:64], total[:, 128:192]], axis=1)
    upper = jnp.concatenate([total[:, 64:128], total[:, 192:256]], axis=1)
    dout[...] = jnp.where(is_low, upper, lower).astype(BF16)
    cp.start(("pair",), dout, dback, at_partner)
    keep = jnp.where(is_low, lower, upper)
    cp.arrived(("pair",))
    gkv[:, core, y] = (keep + dback[...].astype(F32)).astype(BF16).reshape(CHUNKS, 16, 128)
    agr1("w", gkv)
    agr3("q", gq)
    agr2("w", gkv)
    rsc_second("m", f2.at[0], n1.at[0])
    agr3("w", gkv)
    rsc_third("m", n1.at[0], n2.at[0])
    agr_end("q")
    agr_end("w")
    mixed_out = rsc_last("m", n2.at[0], mixed, 0)
    rsc_left("m")
    rsc_far("x", make_gtokens, f1.at[1])
    rsc_near("x", make_gtokens, f1.at[1], f2.at[1], False)
    rsc_own(make_gtokens)
    rsc_near("x", make_gtokens, f1.at[1], f2.at[1], True)
    grad_w_in()
    rsc_second("x", f2.at[1], n1.at[1])
    rsc_third("x", n1.at[1], n2.at[1])
    tokens_out = rsc_last("x", n2.at[1], gtokens, 1)
    for copy in mixed_out + tokens_out:
        copy.wait()
    for n in range(hn // TILE):
        rows = pl.ds(n * TILE, TILE)
        pltpu.make_async_copy(wo.at[rows], gwo.at[rows], out_sem.at[4 + n]).wait()
    for n in range(width // TILE):
        rows = pl.ds(n * TILE, TILE)
        pltpu.make_async_copy(wq.at[rows], gwq.at[rows], out_sem.at[12 + n]).wait()
    pltpu.make_async_copy(wk, gwk, local.at[1]).wait()
    pltpu.make_async_copy(wv, gwv, local.at[2]).wait()
    cp.finish()


def shards(tokens, segment_ids, w_query, w_key, value_weight, w_out, grad_out):
    width = tokens.shape[1]
    hn = w_query.shape[1]
    heads = hn // HEAD
    row = lax.axis_index("row")
    place = (segment_ids * 1024 + jnp.arange(1024, dtype=jnp.int32)).reshape(4, 4, 2, 32)
    order = jnp.stack([place[:, :, 0].transpose(1, 0, 2), place[:, :, 1]])
    order = order.reshape(CHUNKS, 2, 4, 16)
    mrow = order.reshape(1, 1024)
    mcol = lax.dynamic_slice(order, (0, row % 2, row // 2, 0), (CHUNKS, 1, 1, 16)).reshape(128, 1)

    def vm(shape, dtype=BF16):
        return pltpu.VMEM(shape, dtype)

    def rs_scratch(n):
        return [
            vm((2, CHUNKS, 4, 16, n), F32),
            vm((CHUNKS, 4, 16, n), F32),
            vm((2, CHUNKS, 8, n), F32),
            vm((2, CHUNKS, 16, n), F32),
        ]

    scratch = [
        vm((2, 4, 4, 32, width)),
        vm((2, 4, 4, 32, width)),
        vm((width, hn)),
        vm((width, 64)),
        vm((width, 64)),
        vm((width, 128)),
        vm((hn, width)),
        *rs_scratch(hn + 128),
        *rs_scratch(hn),
        *rs_scratch(2 * HEAD),
        vm((CHUNKS, 16, hn)),
        vm((CHUNKS, 16, 128)),
        vm((CHUNKS, 16, 128)),
        vm((CHUNKS, 16, hn)),
        vm((CHUNKS, 2, 4, 16, 2 * HEAD)),
        vm((128, 1024), jnp.int32),
        vm((heads, 128, 1024), F32),
        vm((HEAD, 1024), F32),
        vm((HEAD, 1024), F32),
        vm((CHUNKS, 16, 2 * HEAD), F32),
        vm((128, 128)),
        vm((128, 128)),
        vm((CHUNKS, 2, 4, 16, hn)),
        vm((CHUNKS, 2, 4, 16, hn)),
        vm((CHUNKS, 2, 4, 16, 128)),
        vm((2, 4, 32, width)),
        vm((2, 2, 4, 32, width)),
        vm((2, 4, 32, width), F32),
        vm((2, 2, 2, 2, 32, width)),
        vm((2, 2, 2, 4, 32, width)),
        vm((2, 2, 2, 16, width)),
        vm((2, 2, 2, 32, width)),
        vm((2, 32, width)),
        vm((2, 2, 32, width)),
        vm((2, 2, 32, width)),
        pltpu.SemaphoreType.DMA((SEMS,)),
        pltpu.SemaphoreType.DMA((SEMS,)),
        pltpu.SemaphoreType.DMA((8,)),
        pltpu.SemaphoreType.DMA((20,)),
    ]
    anywhere = pl.BlockSpec(memory_space=pl.ANY)
    inside = pl.BlockSpec(memory_space=pltpu.VMEM)
    shape = jax.ShapeDtypeStruct
    return pl.pallas_call(
        kernel,
        out_shape=(
            shape((64, width), BF16),
            shape((64, width), BF16),
            shape((width, hn), BF16),
            shape((width, 64), BF16),
            shape((width, 64), BF16),
            shape((hn, width), BF16),
        ),
        in_specs=[anywhere] * 6 + [inside] * 2,
        out_specs=(anywhere,) * 6,
        scratch_shapes=scratch,
        compiler_params=pltpu.CompilerParams(
            collective_id=0, has_side_effects=True, vmem_limit_bytes=VMEM_LIMIT
        ),
    )(tokens, grad_out, w_query, w_key, value_weight, w_out, mrow, mcol)


def solution(mesh):
    placed = (
        P("col", "row"),
        P(),
        P("row", "col"),
        P("row", "col"),
        P("row", "col"),
        P("col", "row"),
        P("col", "row"),
    )
    return jax.shard_map(
        shards,
        mesh=mesh,
        in_specs=placed,
        out_specs=(
            P("col", "row"),
            P("col", "row"),
            P("row", "col"),
            P("row", "col"),
            P("row", "col"),
            P("col", "row"),
        ),
        check_vma=False,
    )
```

```python
import jax
import jax.numpy as jnp
from jax import lax
from jax.experimental import pallas as pl
from jax.experimental.pallas import tpu as pltpu
from jax.sharding import PartitionSpec as P

HEAD = 128
CHUNKS = 8
TILE = 256
MESH = pl.DeviceIdType.MESH
F32 = jnp.float32
BF16 = jnp.bfloat16


def nn(left, right):
    return jnp.dot(left, right, preferred_element_type=F32)


def nt(left, right):
    return lax.dot_general(left, right, (((1,), (1,)), ((), ())), preferred_element_type=F32)


def tn(left, right):
    return lax.dot_general(left, right, (((0,), (0,)), ((), ())), preferred_element_type=F32)


def ring(value, step):
    return lax.rem(value + (step + 4), 4)


class Copies:
    def __init__(self, send, recv):
        self.send, self.recv = send, recv
        self.made = {}
        self.sent = set()
        self.here = set()

    def start(self, key, src, dst, device):
        index = len(self.made)
        copy = pltpu.make_async_remote_copy(
            src_ref=src,
            dst_ref=dst,
            send_sem=self.send.at[index],
            recv_sem=self.recv.at[index],
            device_id=device,
            device_id_type=MESH,
        )
        copy.start()
        self.made[key] = copy

    def arrived(self, *keys):
        for key in keys:
            if key not in self.here:
                self.made[key].wait_recv()
                self.here.add(key)

    def left(self, *keys):
        for key in keys:
            if key not in self.sent:
                self.made[key].wait_send()
                self.sent.add(key)

    def finish(self):
        self.arrived(*list(self.made))
        self.left(*list(self.made))


SEMS = 200
STOP = None
VMEM_LIMIT = 64 * 2**20


def kernel(
    tokens, grad_out, wq_in, wk_in, wv_in, wo_in, segments,
    mixed, gtokens, gwq, gwk, gwv, gwo,
    tok, grd, wq, wkv, wo,
    pt, xt, r1t, r2t, pg, xg, lowg, r1g, r2g, pd, xd, r1d, r2d,
    qr, kvp, kvo, gh, kv, mask, probs, dkt, dvt, dsum, dout, dback, dkeep,
    att, gq, gkv,
    stfar, stnear, own, f1, f2, n1, n2, pfar, pnear, outst,
    send, recv, local, out_sem,
):
    row, col = lax.axis_index("row"), lax.axis_index("col")
    y, core = row // 2, lax.rem(row, 2)
    x, z = col // 4, lax.rem(col, 4)
    width = tok.shape[-1]
    heads = qr.shape[-1] // HEAD
    hn = heads * HEAD
    scale = HEAD ** (-0.5)

    def at_x(step):
        return {"col": ring(x, step) * 4 + z}

    def at_z(step):
        return {"col": x * 4 + ring(z, step)}

    def at_y(step):
        return {"row": ring(y, step) * 2 + core}

    at_core = {"row": y * 2 + (1 - core)}
    odd = lax.rem(z, 2)
    at_partner = {"col": x * 4 + (z + 1 - 2 * odd)}

    loads = []

    def load(src, dst):
        loads.append(pltpu.make_async_copy(src, dst, local.at[len(loads)]))

    for n in range(4):
        part = slice(n * width // 4, (n + 1) * width // 4)
        load(wq_in.at[part], wq.at[part])
    load(wk_in, wkv.at[0:64])
    load(wv_in, wkv.at[64:128])
    for n in range(4):
        part = slice(n * hn // 4, (n + 1) * hn // 4)
        load(wo_in.at[part], wo.at[part])
    leaving = []
    half = 32
    own_copies = []
    for n, (src, buf) in enumerate(((tokens, tok), (grad_out, grd))):
        own_copies.append(
            [
                pltpu.make_async_copy(src.at[0:half], buf.at[0, z, x], local.at[10 + 2 * n]),
                pltpu.make_async_copy(src.at[half:], buf.at[1, x, z], local.at[11 + 2 * n]),
            ]
        )
    for pair in own_copies:
        for copy in pair:
            copy.start()
            leaving.append(copy)
    for copy in loads:
        copy.start()
        leaving.append(copy)

    barrier = pltpu.get_barrier_semaphore()
    row_peers = [at_core] + [
        {"row": ring(y, d) * 2 + c} for d in (1, -1, 2) for c in (core, 1 - core)
    ]
    peers = [at_x(1), at_x(-1), at_z(1), at_z(-1)] + row_peers
    for device in peers:
        pl.semaphore_signal(barrier, inc=1, device_id=device, device_id_type=MESH)
    pl.semaphore_wait(barrier, len(peers))

    cp = Copies(send, recv)

    def axes(h):
        return ((at_x, x), (at_z, z)) if h == 0 else ((at_z, z), (at_x, x))

    def ag1(name, src, buf):
        for h in range(2):
            (first, f), (_, s) = axes(h)
            for d in (1, -1):
                cp.start((name, 1, h, d), src.at[h * half : (h + 1) * half], buf.at[h, s, f], first(d))

    def ag1b(name, buf):
        for h in range(2):
            (first, f), (_, s) = axes(h)
            cp.arrived((name, 1, h, 1), (name, 1, h, -1))
            for d, lo in ((1, 0), (-1, 16)):
                part = buf.at[h, s, ring(f, -d), lo : lo + 16]
                cp.start((name, 2, h, d), part, part, first(d))

    def ag2(name, buf):
        for h in range(2):
            cp.arrived((name, 2, h, 1), (name, 2, h, -1))
        for first in (True, False):
            for h in range(2):
                _, (second, s) = axes(h)
                for d in (1, -1):
                    lo = 0 if first == (d == 1) else 2
                    part = buf.at[h, s, lo : lo + 2]
                    cp.start((name, 3, h, d, first), part, part, second(d))

    def ag2b(name, buf):
        for h in range(2):
            _, (second, s) = axes(h)
            cp.arrived((name, 3, h, 1, True), (name, 3, h, -1, True))
            for d, lo in ((1, 0), (-1, 2)):
                part = buf.at[h, ring(s, -d), lo : lo + 2]
                cp.start((name, 4, h, d), part, part, second(d))

    def ag2_end(name):
        for h in range(2):
            cp.arrived((name, 3, h, 1, False), (name, 3, h, -1, False))

    def ag_end(name):
        for h in range(2):
            cp.arrived((name, 4, h, 1), (name, 4, h, -1))

    steps = ((0, 0), (-1, 1), (1, -1), (2, 2))
    pairs = [(ring(z, s), ring(x, s)) for s in (0, 1, -1, 2)]

    def load_pair(buf, p):
        parts = []
        for h, at in enumerate((z, x)):
            for c in range(2):
                part = buf[h, ring(at, steps[p][c]), 2 * c : 2 * c + 2]
                parts.append(part.reshape(64, width))
        return jnp.concatenate(parts, axis=0)

    def put_partial(dst, p, value, columns):
        size = value.shape[-1]
        five = value.reshape(2, 2, 4, 16, size)
        for h in range(2):
            for c in range(2):
                dst[c, 2 * p + h, :, :, columns] = five[h, c]

    def project(p):
        def body(n, carry):
            cols = pl.ds(pl.multiple_of(n * 512, 512), 512)
            put_partial(pt, p, nn(load_pair(tok, p), wq[:, cols]), cols)
            return carry

        lax.fori_loop(0, hn // 512, body, 0)
        put_partial(pt, p, nt(load_pair(tok, p), wkv[...]), pl.ds(hn, 128))

    def project_grad(p):
        def body(n, carry):
            cols = pl.ds(pl.multiple_of(n * 512, 512), 512)
            put_partial(pg, p, nt(load_pair(grd, p), wo[cols, :]), cols)
            return carry

        lax.fori_loop(0, hn // 512, body, 0)

    def rs_core(name, part, held, s0, n):
        cp.start(
            (name, "c", s0), part.at[1 - core, pl.ds(s0, n)], held.at[pl.ds(s0, n)], at_core
        )

    def rs_y1(name, part, held, r1, s0, n):
        cp.arrived((name, "c", s0))
        for s in range(s0, s0 + n):
            held[s] = held[s] + part[core, s]
        for i, d in enumerate((1, -1)):
            cp.start(
                (name, "y1", s0, d),
                held.at[pl.ds(s0, n), ring(y, 2), 8 * i : 8 * i + 8],
                r1.at[i, pl.ds(s0, n)],
                at_y(d),
            )

    def rs_y2(name, held, r1, r2, s0, n):
        cp.arrived((name, "y1", s0, 1), (name, "y1", s0, -1))
        for i, d in enumerate((1, -1)):
            t = ring(y, d)
            lo = 8 * i
            for s in range(s0, s0 + n):
                held[s, t, lo : lo + 8] = held[s, t, lo : lo + 8] + r1[i, s]
            cp.start(
                (name, "y2", s0, d), held.at[pl.ds(s0, n), t], r2.at[i, pl.ds(s0, n)], at_y(d)
            )

    def rs_y1_low(name, part, held, low, r1, s0, n):
        cp.arrived((name, "c", s0))
        far = ring(y, 2)
        cut = held.shape[-1] // 2
        for s in range(s0, s0 + n):
            held[s] = held[s] + part[core, s]
            low[s, far] = held[s, far].astype(BF16)
        for i, d in enumerate((1, -1)):
            cp.start(
                (name, "y1", s0, d),
                low.at[pl.ds(s0, n), far, :, i * cut : (i + 1) * cut],
                r1.at[i, pl.ds(s0, n)],
                at_y(d),
            )

    def rs_y2_low(name, held, low, r1, r2, s0, n):
        cp.arrived((name, "y1", s0, 1), (name, "y1", s0, -1))
        cut = held.shape[-1] // 2
        for i, d in enumerate((1, -1)):
            t = ring(y, d)
            mid = slice(i * cut, (i + 1) * cut)
            rest = slice((1 - i) * cut, (2 - i) * cut)
            for s in range(s0, s0 + n):
                low[s, t, :, mid] = (held[s, t, :, mid] + r1[i, s].astype(F32)).astype(BF16)
                low[s, t, :, rest] = held[s, t, :, rest].astype(BF16)
            cp.start(
                (name, "y2", s0, d), low.at[pl.ds(s0, n), t], r2.at[i, pl.ds(s0, n)], at_y(d)
            )

    def rs_wait(name, s0):
        cp.arrived((name, "y2", s0, 1), (name, "y2", s0, -1))

    def rs_value(held, r2, s):
        return held[s, y] + r2[0, s].astype(F32) + r2[1, s].astype(F32)

    def chunk_of(slot):
        low, high = steps[slot // 2]
        step = low + (high - low) * core
        return ring(z, step) if slot % 2 == 0 else 4 + ring(x, step)

    def fin_tokens(s0, n):
        rs_wait("t", s0)
        for s in range(s0, s0 + n):
            total = rs_value(xt, r2t, s).astype(BF16)
            qr[chunk_of(s)] = total[:, :hn]
            kvp[chunk_of(s)] = total[:, hn:]

    def fin_grads(s0, n):
        rs_wait("g", s0)
        for s in range(s0, s0 + n):
            gh[chunk_of(s)] = rs_value(xg, r2g, s).astype(BF16)

    def cut_of(buf, part):
        if part is None:
            return slice(None)
        size = buf.shape[-1] // 2
        return pl.ds(part * size, size)

    def agr1(name, buf, part):
        mine = buf.at[:, core, y, :, cut_of(buf, part)]
        for d in (1, -1):
            cp.start((name, "a", d), mine, mine, at_y(d))
        cp.start((name, "b", 0), mine, mine, at_core)

    def agr2(name, buf, part):
        cut = cut_of(buf, part)
        cp.arrived((name, "a", 1), (name, "a", -1))
        for d, lo in ((1, 0), (-1, 4)):
            block = buf.at[lo : lo + 4, core, ring(y, -d), :, cut]
            cp.start((name, "c", d), block, block, at_y(d))
        for d in (1, -1):
            block = buf.at[:, core, ring(y, -d), :, cut]
            cp.start((name, "b", d), block, block, at_core)

    def agr3(name, buf, part):
        cp.arrived((name, "c", 1), (name, "c", -1))
        block = buf.at[:, core, ring(y, 2), :, cut_of(buf, part)]
        cp.start((name, "b", 2), block, block, at_core)

    def agr_end(name):
        cp.arrived(*[(name, "b", k) for k in (0, 1, -1, 2)])

    def spread(name, buf):
        mine = buf.at[:, core, y]
        for n, device in enumerate(row_peers):
            cp.start((name, n), mine, mine, device)

    def spread_end(name):
        cp.arrived(*[(name, n) for n in range(len(row_peers))])

    def reuse(name, keys_):
        if name == "x":
            cp.left(*[("m", *key) for key in keys_])

    def rsc_far(name, make, w1):
        def put(k, cols, v):
            stfar[k // 2, pl.ds(2 * (k % 2), 2), :, cols] = v.astype(BF16)

        reuse(name, [("f", h, d) for h in range(2) for d in (1, -1)])
        make(
            [(0, pairs[3][0], 0), (0, pairs[3][0], 1), (1, pairs[3][1], 0), (1, pairs[3][1], 1)],
            put,
        )
        for h in range(2):
            _, (second, _) = axes(h)
            for i, d in enumerate((1, -1)):
                cp.start((name, "f", h, d), stfar.at[h, 2 * i : 2 * i + 2], w1.at[h, i], second(d))

    def near_list(dep):
        items = []
        for h in range(2):
            for i in range(2):
                part = i if dep else 1 - i
                items.append((h, pairs[1 + i][h], part))
        return items

    def rsc_near(name, make, w1, w2, dep):
        if dep:
            for h in range(2):
                cp.arrived((name, "f", h, 1), (name, "f", h, -1))

        def put(k, cols, v):
            h, i = k // 2, k % 2
            part = i if dep else 1 - i
            if dep:
                v = v + w1[h, i, :, :, cols].astype(F32)
            stnear[h, i, pl.ds(2 * part, 2), :, cols] = v.astype(BF16)

        reuse(name, [("n", h, d, e) for h in range(2) for d in (1, -1) for e in (False, True)])
        make(near_list(dep), put)
        for h in range(2):
            _, (second, _) = axes(h)
            for i, d in enumerate((1, -1)):
                part = i if dep else 1 - i
                cp.start(
                    (name, "n", h, d, dep),
                    stnear.at[h, i, 2 * part : 2 * part + 2],
                    w2.at[h, i, 2 * part : 2 * part + 2],
                    second(d),
                )

    def rsc_own(make):
        def put(k, cols, v):
            own[k // 2, pl.ds(2 * (k % 2), 2), :, cols] = v

        make(
            [(0, pairs[0][0], 0), (0, pairs[0][0], 1), (1, pairs[0][1], 0), (1, pairs[0][1], 1)],
            put,
        )

    def rsc_second(name, w2, v1):
        for h in range(2):
            (first, f), _ = axes(h)
            cp.arrived(*[(name, "n", h, d, dep) for d in (1, -1) for dep in (False, True)])
            for s in range(4):
                own[h, s] = own[h, s] + w2[h, 0, s].astype(F32) + w2[h, 1, s].astype(F32)
            reuse(name, [("p", h, 1), ("p", h, -1)])
            pfar[h] = own[h, ring(f, 2)].astype(BF16)
            for i, d in enumerate((1, -1)):
                cp.start((name, "p", h, d), pfar.at[h, 16 * i : 16 * i + 16], v1.at[h, i], first(d))

    def rsc_third(name, v1, v2):
        for h in range(2):
            (first, f), _ = axes(h)
            cp.arrived((name, "p", h, 1), (name, "p", h, -1))
            reuse(name, [("q", h, 1), ("q", h, -1)])
            for i, d in enumerate((1, -1)):
                t = ring(f, d)
                lo = 16 * i
                pnear[h, i, 16 - lo : 32 - lo] = own[h, t, 16 - lo : 32 - lo].astype(BF16)
                pnear[h, i, lo : lo + 16] = (
                    own[h, t, lo : lo + 16] + v1[h, i].astype(F32)
                ).astype(BF16)
                cp.start((name, "q", h, d), pnear.at[h, i], v2.at[h, i], first(d))

    def rsc_last(name, v2, dst, slot):
        for h in range(2):
            (_, f), _ = axes(h)
            cp.arrived((name, "q", h, 1), (name, "q", h, -1))
            outst[slot, h] = (
                own[h, f] + v2[h, 0].astype(F32) + v2[h, 1].astype(F32)
            ).astype(BF16)
            copy = pltpu.make_async_copy(
                outst.at[slot, h], dst.at[h * half : (h + 1) * half], out_sem.at[2 * slot + h]
            )
            copy.start()
            leaving.append(copy)

    def rows_of(buf, items):
        return jnp.concatenate(
            [buf[4 * h + b, c].reshape(64, buf.shape[-1]) for h, b, c in items], axis=0
        )

    def make_mixed(items, put):
        def body(n, carry):
            cols = pl.ds(pl.multiple_of(n * 1024, 1024), 1024)
            v = nn(rows_of(att, items), wo[:, cols]).reshape(4, 2, 32, 1024)
            for k in range(4):
                put(k, cols, v[k])
            return carry

        lax.fori_loop(0, width // 1024, body, 0)

    def make_gtokens(items, put):
        def body(n, carry):
            cols = pl.ds(pl.multiple_of(n * 1024, 1024), 1024)
            v = nt(rows_of(gq, items), wq[cols, :]) + nn(rows_of(gkv, items), wkv[:, cols])
            v = v.reshape(4, 2, 32, 1024)
            for k in range(4):
                put(k, cols, v[k])
            return carry

        lax.fori_loop(0, width // 1024, body, 0)

    def keys():
        return kv[:, :, :, :, 0:HEAD].reshape(1024, HEAD)

    def vals():
        return kv[:, :, :, :, HEAD : 2 * HEAD].reshape(1024, HEAD)

    def place(p):
        i, s, b, h = p & 31, (p >> 5) & 3, (p >> 7) & 3, p >> 9
        xs = jnp.where(h == 0, s, b)
        zs = jnp.where(h == 0, b, s)
        return xs * 256 + zs * 64 + h * 32 + i

    def make_mask():
        seg = segments[...].astype(F32)
        seg = jnp.concatenate([seg[n : n + 1] for n in range(8)], axis=1)
        shape = (1024, 1024)
        key_place = place(lax.broadcasted_iota(jnp.int32, (1, 1024), 1))
        pick = lax.broadcasted_iota(jnp.int32, shape, 0) == key_place
        key_seg = nn(
            jnp.broadcast_to(seg, (16, 1024)).astype(BF16), pick.astype(F32).astype(BF16)
        )[0:1]
        r = lax.broadcasted_iota(jnp.int32, (128, 1), 0)
        mine = place(((r >> 4) << 7) + core * 64 + y * 16 + (r & 15))
        here = lax.broadcasted_iota(jnp.int32, (128, 1024), 1) == mine
        my_seg = jnp.sum(jnp.where(here, seg, F32(0)), axis=1, keepdims=True)
        mask[...] = ((my_seg == key_seg) & (key_place <= mine)).astype(jnp.int32)

    def attend(part):
        def body(h, carry):
            cols = pl.ds(pl.multiple_of(h * HEAD, HEAD), HEAD)
            q = qr[:, :, cols].reshape(128, HEAD)
            s = nt(q, keys()) * scale
            s = jnp.where(mask[...] > 0, s, F32(-1e30))
            e = jnp.exp(s - jnp.max(s, axis=-1, keepdims=True))
            p = e / jnp.sum(e, axis=-1, keepdims=True)
            probs[h] = p
            o = nn(p.astype(BF16), vals()).astype(BF16)
            att[:, core, y, :, cols] = o.reshape(CHUNKS, 16, HEAD)
            return carry

        lax.fori_loop(part * heads // 4, (part + 1) * heads // 4, body, 0)

    def attend_back(part):
        if part == 0:
            dkt[...] = jnp.zeros_like(dkt)
            dvt[...] = jnp.zeros_like(dvt)

        def body(h, carry):
            cols = pl.ds(pl.multiple_of(h * HEAD, HEAD), HEAD)
            q = qr[:, :, cols].reshape(128, HEAD)
            g = gh[:, :, cols].reshape(128, HEAD)
            p = probs[h]
            dp = nt(g, vals())
            inner = jnp.sum(p * dp, axis=-1, keepdims=True)
            ds = (p * (dp - inner) * scale).astype(BF16)
            probs[h] = ds.astype(F32)
            dkt[...] += nn(q.T, ds)
            dvt[...] += nn(g.T, p.astype(BF16))
            return carry

        lax.fori_loop(part * heads // 4, (part + 1) * heads // 4, body, 0)

    def grad_query(part):
        def body(h, carry):
            cols = pl.ds(pl.multiple_of(h * HEAD, HEAD), HEAD)
            dq = nn(probs[h].astype(BF16), keys()).astype(BF16)
            gq[:, core, y, :, cols] = dq.reshape(CHUNKS, 16, HEAD)
            return carry

        lax.fori_loop(part * heads // 2, (part + 1) * heads // 2, body, 0)

    def put_dkv():
        for lo, src in ((0, dkt), (HEAD, dvt)):
            for n in range(CHUNKS):
                block = src[:, n * 128 : (n + 1) * 128].T.reshape(2, 4, 16, HEAD)
                for c in range(2):
                    pd[c, n, :, :, lo : lo + HEAD] = block[c]

    def grad_w_out(part):
        size = hn // 4
        rows = slice(part * size, (part + 1) * size)

        def body(m, carry):
            cols = pl.ds(pl.multiple_of(m * 1024, 1024), 1024)
            left = att[:, :, :, :, rows].reshape(1024, size)
            wo[rows, cols] = tn(left, grd[:, :, :, :, cols].reshape(1024, 1024)).astype(BF16)
            return carry

        lax.fori_loop(0, width // 1024, body, 0)
        copy = pltpu.make_async_copy(wo.at[rows], gwo.at[rows], out_sem.at[4 + part])
        copy.start()
        leaving.append(copy)

    def grad_w_in(part):
        size = width // 4
        rows = slice(part * size, (part + 1) * size)

        def body(m, carry):
            cols = pl.ds(pl.multiple_of(m * 512, 512), 512)
            left = tok[:, :, :, :, rows].reshape(1024, size)
            wq[rows, cols] = tn(left, gq[:, :, :, :, cols].reshape(1024, 512)).astype(BF16)
            return carry

        lax.fori_loop(0, hn // 512, body, 0)
        left = tok[:, :, :, :, rows].reshape(1024, size)
        wkv[:, rows] = tn(gkv[...].reshape(1024, 128), left).astype(BF16)
        moves = [(wq.at[rows], gwq.at[rows])]
        if part == 3:
            moves += [(wkv.at[0:64], gwk), (wkv.at[64:128], gwv)]
        for n, (src, dst) in enumerate(moves):
            copy = pltpu.make_async_copy(src, dst, out_sem.at[8 + part + n])
            copy.start()
            leaving.append(copy)

    is_low = jnp.full((128, 128), odd, jnp.int32) == 0

    def wait_local(copies):
        for copy in copies:
            copy.wait()
            leaving[:] = [c for c in leaving if c is not copy]

    def join_start():
        cp.start(("kv",), kvp, kvo, at_partner)

    def join_end():
        cp.arrived(("kv",))
        mine, other = kvp[...].reshape(128, 128), kvo[...].reshape(128, 128)
        low = jnp.where(is_low, mine, other)
        high = jnp.where(is_low, other, mine)
        joined = jnp.concatenate([low[:, :64], high[:, :64], low[:, 64:], high[:, 64:]], axis=1)
        kv[:, core, y] = joined.reshape(CHUNKS, 16, 2 * HEAD)

    def split_start():
        rs_wait("d", 0)
        for n in range(CHUNKS):
            dsum[n] = rs_value(xd, r2d, n)
        total = dsum[...].reshape(128, 2 * HEAD)
        lower = jnp.concatenate([total[:, 0:64], total[:, 128:192]], axis=1)
        upper = jnp.concatenate([total[:, 64:128], total[:, 192:256]], axis=1)
        dout[...] = jnp.where(is_low, upper, lower).astype(BF16)
        cp.start(("pair",), dout, dback, at_partner)
        dkeep[...] = jnp.where(is_low, lower, upper)

    def split_end():
        cp.arrived(("pair",))
        kept = (dkeep[...] + dback[...].astype(F32)).astype(BF16)
        gkv[:, core, y] = kept.reshape(CHUNKS, 16, 128)

    work = [
        (ag1, "t", tokens, tok),
        (wait_local, own_copies[0]),
        (ag1, "g", grad_out, grd),
        (wait_local, own_copies[1]),
        (make_mask,),
        (wait_local, loads[0:6]),
        (ag1b, "t", tok),
        (wait_local, loads[6:]),
        (ag1b, "g", grd),
        (ag2, "t", tok),
        (project, 0),
        (rs_core, "t", pt, xt, 0, 2),
        (rs_y1, "t", pt, xt, r1t, 0, 2),
        (ag2b, "t", tok),
        (ag2, "g", grd),
        (rs_y2, "t", xt, r1t, r2t, 0, 2),
        (project, 1),
        (rs_core, "t", pt, xt, 2, 2),
        (project_grad, 0),
        (rs_core, "g", pg, xg, 0, 2),
        (rs_y1, "t", pt, xt, r1t, 2, 2),
        (fin_tokens, 0, 2),
        (ag2_end, "t"),
        (project, 2),
        (rs_core, "t", pt, xt, 4, 2),
        (rs_y1_low, "g", pg, xg, lowg, r1g, 0, 2),
        (rs_y2, "t", xt, r1t, r2t, 2, 2),
        (rs_y1, "t", pt, xt, r1t, 4, 2),
        (rs_y2_low, "g", xg, lowg, r1g, r2g, 0, 2),
        (ag_end, "t"),
        (project, 3),
        (rs_core, "t", pt, xt, 6, 2),
        (fin_tokens, 2, 2),
        (rs_y2, "t", xt, r1t, r2t, 4, 2),
        (rs_y1, "t", pt, xt, r1t, 6, 2),
        (fin_grads, 0, 2),
        (ag2b, "g", grd),
        (project_grad, 1),
        (rs_core, "g", pg, xg, 2, 2),
        (fin_tokens, 4, 2),
        (rs_y2, "t", xt, r1t, r2t, 6, 2),
        (rs_y1_low, "g", pg, xg, lowg, r1g, 2, 2),
        (ag2_end, "g"),
        (project_grad, 2),
        (rs_core, "g", pg, xg, 4, 2),
        (fin_tokens, 6, 2),
        (join_start,),
        (rs_y2_low, "g", xg, lowg, r1g, r2g, 2, 2),
        (rs_y1_low, "g", pg, xg, lowg, r1g, 4, 2),
        (join_end,),
        (agr1, "k", kv, None),
        (ag_end, "g"),
        (project_grad, 3),
        (rs_core, "g", pg, xg, 6, 2),
        (rs_y2_low, "g", xg, lowg, r1g, r2g, 4, 2),
        (fin_grads, 2, 2),
        (agr2, "k", kv, None),
        (rs_y1_low, "g", pg, xg, lowg, r1g, 6, 2),
        (fin_grads, 4, 2),
        (agr3, "k", kv, None),
        (rs_y2_low, "g", xg, lowg, r1g, r2g, 6, 2),
        (agr_end, "k"),
        (attend, 0),
        (attend, 1),
        (agr1, "o0", att, 0),
        (fin_grads, 6, 2),
        (attend, 2),
        (attend, 3),
        (agr1, "o1", att, 1),
        (attend_back, 0),
        (agr2, "o0", att, 0),
        (attend_back, 1),
        (attend_back, 2),
        (agr3, "o0", att, 0),
        (agr2, "o1", att, 1),
        (attend_back, 3),
        (agr_end, "o0"),
        (put_dkv,),
        (rs_core, "d", pd, xd, 0, 8),
        (agr3, "o1", att, 1),
        (grad_query, 0),
        (agr1, "q0", gq, 0),
        (grad_query, 1),
        (agr1, "q1", gq, 1),
        (rs_y1, "d", pd, xd, r1d, 0, 8),
        (agr_end, "o1"),
        (rsc_far, "m", make_mixed, f1.at[0]),
        (rsc_near, "m", make_mixed, f1.at[0], f2.at[0], False),
        (agr2, "q0", gq, 0),
        (rsc_own, make_mixed),
        (agr2, "q1", gq, 1),
        (rs_y2, "d", xd, r1d, r2d, 0, 8),
        (agr3, "q0", gq, 0),
        (rsc_near, "m", make_mixed, f1.at[0], f2.at[0], True),
        (agr_end, "q0"),
        (agr3, "q1", gq, 1),
        (grad_w_out, 0),
        (agr_end, "q1"),
        (grad_w_out, 1),
        (split_start,),
        (grad_w_out, 2),
        (grad_w_out, 3),
        (split_end,),
        (spread, "w", gkv),
        (rsc_second, "m", f2.at[0], n1.at[0]),
        (spread_end, "w"),
        (rsc_far, "x", make_gtokens, f1.at[1]),
        (rsc_third, "m", n1.at[0], n2.at[0]),
        (rsc_near, "x", make_gtokens, f1.at[1], f2.at[1], False),
        (rsc_near, "x", make_gtokens, f1.at[1], f2.at[1], True),
        (rsc_last, "m", n2.at[0], mixed, 0),
        (rsc_own, make_gtokens),
        (grad_w_in, 0),
        (grad_w_in, 1),
        (grad_w_in, 2),
        (grad_w_in, 3),
        (rsc_second, "x", f2.at[1], n1.at[1]),
        (rsc_third, "x", n1.at[1], n2.at[1]),
        (rsc_last, "x", n2.at[1], gtokens, 1),
    ]
    for step in work[:STOP]:
        step[0](*step[1:])
    wait_local(list(leaving))
    cp.finish()


def hand_over(arrays):
    count = len(arrays)
    pieces = [max(1, a.size // 2**18) for a in arrays]
    total = sum(pieces)

    def body(*refs):
        sources, results, held = refs[:count], refs[count : 2 * count], refs[2 * count : 3 * count]
        came, went = refs[-2:]
        moves = []
        for n in range(count):
            rows = arrays[n].shape[0] // pieces[n]
            for k in range(pieces[n]):
                at, m = pl.ds(k * rows, rows), len(moves)
                moves.append(
                    (
                        pltpu.make_async_copy(sources[n].at[at], held[n].at[at], came.at[m]),
                        pltpu.make_async_copy(held[n].at[at], results[n].at[at], went.at[m]),
                    )
                )
        for come, _ in moves:
            come.start()
        for come, go in moves:
            come.wait()
            go.start()
        for _, go in moves:
            go.wait()

    anywhere = pl.BlockSpec(memory_space=pl.ANY)
    return pl.pallas_call(
        body,
        out_shape=tuple(jax.ShapeDtypeStruct(a.shape, a.dtype) for a in arrays),
        in_specs=[anywhere] * count,
        out_specs=(anywhere,) * count,
        scratch_shapes=[
            *(pltpu.VMEM(a.shape, a.dtype) for a in arrays),
            pltpu.SemaphoreType.DMA((total,)),
            pltpu.SemaphoreType.DMA((total,)),
        ],
        compiler_params=pltpu.CompilerParams(vmem_limit_bytes=32 * 2**20),
    )(*arrays)


def shards(tokens, segment_ids, w_query, w_key, value_weight, w_out, grad_out):
    width = tokens.shape[1]
    hn = w_query.shape[1]
    heads = hn // HEAD
    def vm(shape, dtype=BF16):
        return pltpu.VMEM(shape, dtype)

    def rs_scratch(n):
        return [
            vm((2, CHUNKS, 4, 16, n), F32),
            vm((CHUNKS, 4, 16, n), F32),
            vm((2, CHUNKS, 8, n), F32),
            vm((2, CHUNKS, 16, n), F32),
        ]

    scratch = [
        vm((2, 4, 4, 32, width)),
        vm((2, 4, 4, 32, width)),
        vm((width, hn)),
        vm((128, width)),
        vm((hn, width)),
        *rs_scratch(hn + 128),
        vm((2, CHUNKS, 4, 16, hn), F32),
        vm((CHUNKS, 4, 16, hn), F32),
        vm((CHUNKS, 4, 16, hn)),
        vm((2, CHUNKS, 16, hn // 2)),
        vm((2, CHUNKS, 16, hn)),
        *rs_scratch(2 * HEAD),
        vm((CHUNKS, 16, hn)),
        vm((CHUNKS, 16, 128)),
        vm((CHUNKS, 16, 128)),
        vm((CHUNKS, 16, hn)),
        vm((CHUNKS, 2, 4, 16, 2 * HEAD)),
        vm((128, 1024), jnp.int32),
        vm((heads, 128, 1024), F32),
        vm((HEAD, 1024), F32),
        vm((HEAD, 1024), F32),
        vm((CHUNKS, 16, 2 * HEAD), F32),
        vm((128, 128)),
        vm((128, 128)),
        vm((128, 128), F32),
        vm((CHUNKS, 2, 4, 16, hn)),
        vm((CHUNKS, 2, 4, 16, hn)),
        vm((CHUNKS, 2, 4, 16, 128)),
        vm((2, 4, 32, width)),
        vm((2, 2, 4, 32, width)),
        vm((2, 4, 32, width), F32),
        vm((2, 2, 2, 2, 32, width)),
        vm((2, 2, 2, 4, 32, width)),
        vm((2, 2, 2, 16, width)),
        vm((2, 2, 2, 32, width)),
        vm((2, 32, width)),
        vm((2, 2, 32, width)),
        vm((2, 2, 32, width)),
        pltpu.SemaphoreType.DMA((SEMS,)),
        pltpu.SemaphoreType.DMA((SEMS,)),
        pltpu.SemaphoreType.DMA((16,)),
        pltpu.SemaphoreType.DMA((20,)),
    ]
    anywhere = pl.BlockSpec(memory_space=pl.ANY)
    inside = pl.BlockSpec(memory_space=pltpu.VMEM)
    shape = jax.ShapeDtypeStruct
    made = pl.pallas_call(
        kernel,
        out_shape=(
            shape((64, width), BF16),
            shape((64, width), BF16),
            shape((width, hn), BF16),
            shape((64, width), BF16),
            shape((64, width), BF16),
            shape((hn, width), BF16),
        ),
        in_specs=[anywhere] * 6 + [inside],
        out_specs=(anywhere,) * 6,
        scratch_shapes=scratch,
        compiler_params=pltpu.CompilerParams(
            collective_id=0, has_side_effects=True, vmem_limit_bytes=VMEM_LIMIT
        ),
    )(
        tokens, grad_out, w_query, w_key.T, value_weight.T, w_out, segment_ids.reshape(8, 128)
    )
    mixed, gtokens, gwq, gwk, gwv, gwo = hand_over(made)
    return mixed, gtokens, gwq, gwk.T, gwv.T, gwo


def solution(mesh):
    placed = (
        P("col", "row"),
        P(),
        P("row", "col"),
        P("row", "col"),
        P("row", "col"),
        P("col", "row"),
        P("col", "row"),
    )
    return jax.shard_map(
        shards,
        mesh=mesh,
        in_specs=placed,
        out_specs=(
            P("col", "row"),
            P("col", "row"),
            P("row", "col"),
            P("row", "col"),
            P("row", "col"),
            P("col", "row"),
        ),
        check_vma=False,
    )
```

```python
import jax
import jax.numpy as jnp
from jax import lax
from jax.experimental import pallas as pl
from jax.experimental.pallas import tpu as pltpu
from jax.sharding import PartitionSpec as P

HEAD = 128
CHUNKS = 8
TILE = 256
MESH = pl.DeviceIdType.MESH
F32 = jnp.float32
BF16 = jnp.bfloat16


def nn(left, right):
    return jnp.dot(left, right, preferred_element_type=F32)


def nt(left, right):
    return lax.dot_general(left, right, (((1,), (1,)), ((), ())), preferred_element_type=F32)


def tn(left, right):
    return lax.dot_general(left, right, (((0,), (0,)), ((), ())), preferred_element_type=F32)


def ring(value, step):
    return lax.rem(value + (step + 4), 4)


class Copies:
    def __init__(self, send, recv):
        self.send, self.recv = send, recv
        self.made = {}
        self.sent = set()
        self.here = set()

    def start(self, key, src, dst, device):
        index = len(self.made)
        copy = pltpu.make_async_remote_copy(
            src_ref=src,
            dst_ref=dst,
            send_sem=self.send.at[index],
            recv_sem=self.recv.at[index],
            device_id=device,
            device_id_type=MESH,
        )
        copy.start()
        self.made[key] = copy

    def arrived(self, *keys):
        for key in keys:
            if key not in self.here:
                self.made[key].wait_recv()
                self.here.add(key)

    def left(self, *keys):
        for key in keys:
            if key not in self.sent:
                self.made[key].wait_send()
                self.sent.add(key)

    def finish(self):
        self.arrived(*list(self.made))
        self.left(*list(self.made))


SEMS = 240
STOP = None
VMEM_LIMIT = 64 * 2**20


def kernel(
    tokens, grad_out, wq_in, wk_in, wv_in, wo_in, segments,
    mixed, gtokens, gwq, gwk, gwv, gwo,
    tok, grd, wq, wkv, wo,
    pt, xt, r1t, r2t, pv, xv, r1v, r2v, pg, xg, lowg, r1g, r2g, pd, xd, r1d, r2d,
    qr, kvp, kvo, gh, kv, mask, probs, dkt, dvt, dsum, dout, dback, dkeep,
    att, gq, gkv,
    stfar, stnear, own, f1, f2, n1, n2, pfar, pnear, outst,
    send, recv, local, out_sem,
):
    row, col = lax.axis_index("row"), lax.axis_index("col")
    y, core = row // 2, lax.rem(row, 2)
    x, z = col // 4, lax.rem(col, 4)
    width = tok.shape[-1]
    heads = qr.shape[-1] // HEAD
    hn = heads * HEAD
    scale = HEAD ** (-0.5)

    def at_x(step):
        return {"col": ring(x, step) * 4 + z}

    def at_z(step):
        return {"col": x * 4 + ring(z, step)}

    def at_y(step):
        return {"row": ring(y, step) * 2 + core}

    at_core = {"row": y * 2 + (1 - core)}
    odd = lax.rem(z, 2)
    at_partner = {"col": x * 4 + (z + 1 - 2 * odd)}

    loads = []

    def load(src, dst):
        loads.append(pltpu.make_async_copy(src, dst, local.at[len(loads)]))

    for n in range(4):
        part = slice(n * width // 4, (n + 1) * width // 4)
        load(wq_in.at[part], wq.at[part])
    load(wk_in, wkv.at[0:64])
    load(wv_in, wkv.at[64:128])
    for n in range(4):
        part = slice(n * hn // 4, (n + 1) * hn // 4)
        load(wo_in.at[part], wo.at[part])
    leaving = []
    half = 32
    own_copies = []
    for n, (src, buf) in enumerate(((tokens, tok), (grad_out, grd))):
        own_copies.append(
            [
                pltpu.make_async_copy(src.at[0:half], buf.at[0, z, x], local.at[10 + 2 * n]),
                pltpu.make_async_copy(src.at[half:], buf.at[1, x, z], local.at[11 + 2 * n]),
            ]
        )
    for pair in own_copies:
        for copy in pair:
            copy.start()
            leaving.append(copy)
    for copy in loads:
        copy.start()
        leaving.append(copy)

    barrier = pltpu.get_barrier_semaphore()
    row_peers = [at_core] + [
        {"row": ring(y, d) * 2 + c} for d in (1, -1, 2) for c in (core, 1 - core)
    ]
    peers = [at_x(1), at_x(-1), at_z(1), at_z(-1)] + row_peers
    for device in peers:
        pl.semaphore_signal(barrier, inc=1, device_id=device, device_id_type=MESH)
    pl.semaphore_wait(barrier, len(peers))

    cp = Copies(send, recv)

    def axes(h):
        return ((at_x, x), (at_z, z)) if h == 0 else ((at_z, z), (at_x, x))

    def ag1(name, src, buf):
        for h in range(2):
            (first, f), (_, s) = axes(h)
            for d in (1, -1):
                cp.start((name, 1, h, d), src.at[h * half : (h + 1) * half], buf.at[h, s, f], first(d))

    def ag1b(name, buf):
        for h in range(2):
            (first, f), (_, s) = axes(h)
            cp.arrived((name, 1, h, 1), (name, 1, h, -1))
            for d, lo in ((1, 0), (-1, 16)):
                part = buf.at[h, s, ring(f, -d), lo : lo + 16]
                cp.start((name, 2, h, d), part, part, first(d))

    def ag2(name, buf):
        for h in range(2):
            cp.arrived((name, 2, h, 1), (name, 2, h, -1))
        for first in (True, False):
            for h in range(2):
                _, (second, s) = axes(h)
                for d in (1, -1):
                    lo = 0 if first == (d == 1) else 2
                    part = buf.at[h, s, lo : lo + 2]
                    cp.start((name, 3, h, d, first), part, part, second(d))

    def ag2b(name, buf):
        for h in range(2):
            _, (second, s) = axes(h)
            cp.arrived((name, 3, h, 1, True), (name, 3, h, -1, True))
            for d, lo in ((1, 0), (-1, 2)):
                part = buf.at[h, ring(s, -d), lo : lo + 2]
                cp.start((name, 4, h, d), part, part, second(d))

    def ag2_end(name):
        for h in range(2):
            cp.arrived((name, 3, h, 1, False), (name, 3, h, -1, False))

    def ag_end(name):
        for h in range(2):
            cp.arrived((name, 4, h, 1), (name, 4, h, -1))

    steps = ((0, 0), (-1, 1), (1, -1), (2, 2))
    pairs = [(ring(z, s), ring(x, s)) for s in (0, 1, -1, 2)]

    def load_pair(buf, p):
        parts = []
        for h, at in enumerate((z, x)):
            for c in range(2):
                part = buf[h, ring(at, steps[p][c]), 2 * c : 2 * c + 2]
                parts.append(part.reshape(64, width))
        return jnp.concatenate(parts, axis=0)

    def put_partial(dst, p, value, columns):
        size = value.shape[-1]
        five = value.reshape(2, 2, 4, 16, size)
        for h in range(2):
            for c in range(2):
                dst[c, 2 * p + h, :, :, columns] = five[h, c]

    def project(p):
        def body(n, carry):
            cols = pl.ds(pl.multiple_of(n * 512, 512), 512)
            put_partial(pt, p, nn(load_pair(tok, p), wq[:, cols]), cols)
            return carry

        lax.fori_loop(0, hn // 512, body, 0)

    def project_kv(p):
        put_partial(pv, p, nt(load_pair(tok, p), wkv[...]), pl.ds(0, 128))

    def project_grad(p):
        def body(n, carry):
            cols = pl.ds(pl.multiple_of(n * 512, 512), 512)
            put_partial(pg, p, nt(load_pair(grd, p), wo[cols, :]), cols)
            return carry

        lax.fori_loop(0, hn // 512, body, 0)

    def rs_core(name, part, held, s0, n):
        cp.start(
            (name, "c", s0), part.at[1 - core, pl.ds(s0, n)], held.at[pl.ds(s0, n)], at_core
        )

    def rs_y1(name, part, held, r1, s0, n):
        cp.arrived((name, "c", s0))
        for s in range(s0, s0 + n):
            held[s] = held[s] + part[core, s]
        for i, d in enumerate((1, -1)):
            cp.start(
                (name, "y1", s0, d),
                held.at[pl.ds(s0, n), ring(y, 2), 8 * i : 8 * i + 8],
                r1.at[i, pl.ds(s0, n)],
                at_y(d),
            )

    def rs_y2(name, held, r1, r2, s0, n):
        cp.arrived((name, "y1", s0, 1), (name, "y1", s0, -1))
        for i, d in enumerate((1, -1)):
            t = ring(y, d)
            lo = 8 * i
            for s in range(s0, s0 + n):
                held[s, t, lo : lo + 8] = held[s, t, lo : lo + 8] + r1[i, s]
            cp.start(
                (name, "y2", s0, d), held.at[pl.ds(s0, n), t], r2.at[i, pl.ds(s0, n)], at_y(d)
            )

    def rs_y1_low(name, part, held, low, r1, s0, n):
        cp.arrived((name, "c", s0))
        far = ring(y, 2)
        cut = held.shape[-1] // 2
        for s in range(s0, s0 + n):
            held[s] = held[s] + part[core, s]
            low[s, far] = held[s, far].astype(BF16)
        for i, d in enumerate((1, -1)):
            cp.start(
                (name, "y1", s0, d),
                low.at[pl.ds(s0, n), far, :, i * cut : (i + 1) * cut],
                r1.at[i, pl.ds(s0, n)],
                at_y(d),
            )

    def rs_y2_low(name, held, low, r1, r2, s0, n):
        cp.arrived((name, "y1", s0, 1), (name, "y1", s0, -1))
        cut = held.shape[-1] // 2
        for i, d in enumerate((1, -1)):
            t = ring(y, d)
            mid = slice(i * cut, (i + 1) * cut)
            rest = slice((1 - i) * cut, (2 - i) * cut)
            for s in range(s0, s0 + n):
                low[s, t, :, mid] = (held[s, t, :, mid] + r1[i, s].astype(F32)).astype(BF16)
                low[s, t, :, rest] = held[s, t, :, rest].astype(BF16)
            cp.start(
                (name, "y2", s0, d), low.at[pl.ds(s0, n), t], r2.at[i, pl.ds(s0, n)], at_y(d)
            )

    def rs_wait(name, s0):
        cp.arrived((name, "y2", s0, 1), (name, "y2", s0, -1))

    def rs_value(held, r2, s):
        return held[s, y] + r2[0, s].astype(F32) + r2[1, s].astype(F32)

    def chunk_of(slot):
        low, high = steps[slot // 2]
        step = low + (high - low) * core
        return ring(z, step) if slot % 2 == 0 else 4 + ring(x, step)

    def fin_tokens(s0, n):
        rs_wait("t", s0)
        for s in range(s0, s0 + n):
            qr[chunk_of(s)] = rs_value(xt, r2t, s).astype(BF16)

    def fin_kv(s0, n):
        rs_wait("v", s0)
        for s in range(s0, s0 + n):
            kvp[chunk_of(s)] = rs_value(xv, r2v, s).astype(BF16)

    def fin_grads(s0, n):
        rs_wait("g", s0)
        for s in range(s0, s0 + n):
            gh[chunk_of(s)] = rs_value(xg, r2g, s).astype(BF16)

    def cut_of(buf, part):
        if part is None:
            return slice(None)
        size = buf.shape[-1] // 2
        return pl.ds(part * size, size)

    def agr1(name, buf, part):
        mine = buf.at[:, core, y, :, cut_of(buf, part)]
        for d in (1, -1):
            cp.start((name, "a", d), mine, mine, at_y(d))
        cp.start((name, "b", 0), mine, mine, at_core)

    def agr2(name, buf, part):
        cut = cut_of(buf, part)
        cp.arrived((name, "a", 1), (name, "a", -1))
        for d, lo in ((1, 0), (-1, 4)):
            block = buf.at[lo : lo + 4, core, ring(y, -d), :, cut]
            cp.start((name, "c", d), block, block, at_y(d))
        for d in (1, -1):
            block = buf.at[:, core, ring(y, -d), :, cut]
            cp.start((name, "b", d), block, block, at_core)

    def agr3(name, buf, part):
        cp.arrived((name, "c", 1), (name, "c", -1))
        block = buf.at[:, core, ring(y, 2), :, cut_of(buf, part)]
        cp.start((name, "b", 2), block, block, at_core)

    def agr_end(name):
        cp.arrived(*[(name, "b", k) for k in (0, 1, -1, 2)])

    def spread(name, buf):
        mine = buf.at[:, core, y]
        for n, device in enumerate(row_peers):
            cp.start((name, n), mine, mine, device)

    def spread_end(name):
        cp.arrived(*[(name, n) for n in range(len(row_peers))])

    def reuse(name, keys_):
        if name == "x":
            cp.left(*[("m", *key) for key in keys_])

    cw = width // 2

    def rsc_far(name, make, w1, part):
        cols = slice(part * cw, (part + 1) * cw)
        reuse(name, [("f", h, d, part) for h in range(2) for d in (1, -1)])
        v = make(
            [(0, pairs[3][0], 0), (0, pairs[3][0], 1), (1, pairs[3][1], 0), (1, pairs[3][1], 1)],
            cols,
        )
        for h in range(2):
            _, (second, _) = axes(h)
            for i, d in enumerate((1, -1)):
                stfar[h, 2 * i : 2 * i + 2, :, cols] = v[2 * h + i].astype(BF16)
                cp.start(
                    (name, "f", h, d, part),
                    stfar.at[h, 2 * i : 2 * i + 2, :, cols],
                    w1.at[h, i, :, :, cols],
                    second(d),
                )

    def rsc_near(name, make, w1, w2, dep, part):
        cols = slice(part * cw, (part + 1) * cw)
        items = []
        for h in range(2):
            for i in range(2):
                items.append((h, pairs[1 + i][h], i if dep else 1 - i))
        v = make(items, cols)
        for h in range(2):
            _, (second, _) = axes(h)
            if dep:
                cp.arrived((name, "f", h, 1, part), (name, "f", h, -1, part))
            for i, d in enumerate((1, -1)):
                reuse(name, [("n", h, d, dep, part)])
                at = 2 * i if dep else 2 - 2 * i
                value = v[2 * h + i]
                if dep:
                    value = value + w1[h, i, :, :, cols].astype(F32)
                stnear[h, i, at : at + 2, :, cols] = value.astype(BF16)
                cp.start(
                    (name, "n", h, d, dep, part),
                    stnear.at[h, i, at : at + 2, :, cols],
                    w2.at[h, i, at : at + 2, :, cols],
                    second(d),
                )

    def rsc_own(make, part):
        cols = slice(part * cw, (part + 1) * cw)
        v = make(
            [(0, pairs[0][0], 0), (0, pairs[0][0], 1), (1, pairs[0][1], 0), (1, pairs[0][1], 1)],
            cols,
        )
        for h in range(2):
            for i in range(2):
                own[h, 2 * i : 2 * i + 2, :, cols] = v[2 * h + i]

    def rsc_second(name, w2, v1, part):
        cols = slice(part * cw, (part + 1) * cw)
        for h in range(2):
            (first, f), _ = axes(h)
            cp.arrived(*[(name, "n", h, d, dep, part) for d in (1, -1) for dep in (False, True)])
            for k in (2, 1, -1, 0):
                s = ring(f, k)
                own[h, s, :, cols] = (
                    own[h, s, :, cols]
                    + w2[h, 0, s, :, cols].astype(F32)
                    + w2[h, 1, s, :, cols].astype(F32)
                )
                if k == 2:
                    reuse(name, [("p", h, 1, part), ("p", h, -1, part)])
                    pfar[h, :, cols] = own[h, s, :, cols].astype(BF16)
                    for i, d in enumerate((1, -1)):
                        lo = 16 * i
                        cp.start(
                            (name, "p", h, d, part),
                            pfar.at[h, lo : lo + 16, cols],
                            v1.at[h, i, :, cols],
                            first(d),
                        )

    def rsc_third(name, v1, v2, part):
        cols = slice(part * cw, (part + 1) * cw)
        for h in range(2):
            (first, f), _ = axes(h)
            cp.arrived((name, "p", h, 1, part), (name, "p", h, -1, part))
            reuse(name, [("q", h, 1, part), ("q", h, -1, part)])
            for i, d in enumerate((1, -1)):
                t = ring(f, d)
                mid = slice(16 * i, 16 * i + 16)
                rest = slice(16 - 16 * i, 32 - 16 * i)
                pnear[h, i, rest, cols] = own[h, t, rest, cols].astype(BF16)
                pnear[h, i, mid, cols] = (
                    own[h, t, mid, cols] + v1[h, i, :, cols].astype(F32)
                ).astype(BF16)
                cp.start(
                    (name, "q", h, d, part), pnear.at[h, i, :, cols], v2.at[h, i, :, cols], first(d)
                )

    def rsc_last(name, v2, dst, slot, part):
        cols = slice(part * cw, (part + 1) * cw)
        for h in range(2):
            (_, f), _ = axes(h)
            cp.arrived((name, "q", h, 1, part), (name, "q", h, -1, part))
            outst[slot, h, :, cols] = (
                own[h, f, :, cols]
                + v2[h, 0, :, cols].astype(F32)
                + v2[h, 1, :, cols].astype(F32)
            ).astype(BF16)
            copy = pltpu.make_async_copy(
                outst.at[slot, h, :, cols],
                dst.at[h * half : (h + 1) * half, cols],
                out_sem.at[16 + 4 * slot + 2 * part + h],
            )
            copy.start()
            leaving.append(copy)

    def rows_of(buf, items):
        return jnp.concatenate(
            [buf[4 * h + b, c].reshape(64, buf.shape[-1]) for h, b, c in items], axis=0
        )

    def make_mixed(items, cols):
        return nn(rows_of(att, items), wo[:, cols]).reshape(4, 2, 32, cw)

    def make_gtokens(items, cols):
        v = nt(rows_of(gq, items), wq[cols, :]) + nn(rows_of(gkv, items), wkv[:, cols])
        return v.reshape(4, 2, 32, cw)

    def keys():
        return kv[:, :, :, :, 0:HEAD].reshape(1024, HEAD)

    def vals():
        return kv[:, :, :, :, HEAD : 2 * HEAD].reshape(1024, HEAD)

    def place(p):
        i, s, b, h = p & 31, (p >> 5) & 3, (p >> 7) & 3, p >> 9
        xs = jnp.where(h == 0, s, b)
        zs = jnp.where(h == 0, b, s)
        return xs * 256 + zs * 64 + h * 32 + i

    def make_mask():
        seg = segments[...].astype(F32)
        seg = jnp.concatenate([seg[n : n + 1] for n in range(8)], axis=1)
        shape = (1024, 1024)
        key_place = place(lax.broadcasted_iota(jnp.int32, (1, 1024), 1))
        pick = lax.broadcasted_iota(jnp.int32, shape, 0) == key_place
        key_seg = nn(
            jnp.broadcast_to(seg, (16, 1024)).astype(BF16), pick.astype(F32).astype(BF16)
        )[0:1]
        r = lax.broadcasted_iota(jnp.int32, (128, 1), 0)
        mine = place(((r >> 4) << 7) + core * 64 + y * 16 + (r & 15))
        here = lax.broadcasted_iota(jnp.int32, (128, 1024), 1) == mine
        my_seg = jnp.sum(jnp.where(here, seg, F32(0)), axis=1, keepdims=True)
        mask[...] = ((my_seg == key_seg) & (key_place <= mine)).astype(jnp.int32)

    def attend(part):
        def body(h, carry):
            cols = pl.ds(pl.multiple_of(h * HEAD, HEAD), HEAD)
            q = qr[:, :, cols].reshape(128, HEAD)
            s = nt(q, keys()) * scale
            s = jnp.where(mask[...] > 0, s, F32(-1e30))
            e = jnp.exp(s - jnp.max(s, axis=-1, keepdims=True))
            p = e / jnp.sum(e, axis=-1, keepdims=True)
            probs[h] = p
            o = nn(p.astype(BF16), vals()).astype(BF16)
            att[:, core, y, :, cols] = o.reshape(CHUNKS, 16, HEAD)
            return carry

        lax.fori_loop(part * heads // 4, (part + 1) * heads // 4, body, 0)

    def attend_back(part):
        if part == 0:
            dkt[...] = jnp.zeros_like(dkt)
            dvt[...] = jnp.zeros_like(dvt)

        def body(h, carry):
            cols = pl.ds(pl.multiple_of(h * HEAD, HEAD), HEAD)
            q = qr[:, :, cols].reshape(128, HEAD)
            g = gh[:, :, cols].reshape(128, HEAD)
            p = probs[h]
            dp = nt(g, vals())
            inner = jnp.sum(p * dp, axis=-1, keepdims=True)
            ds = (p * (dp - inner) * scale).astype(BF16)
            probs[h] = ds.astype(F32)
            dkt[...] += nn(q.T, ds)
            dvt[...] += nn(g.T, p.astype(BF16))
            return carry

        lax.fori_loop(part * heads // 4, (part + 1) * heads // 4, body, 0)

    def grad_query(part):
        def body(h, carry):
            cols = pl.ds(pl.multiple_of(h * HEAD, HEAD), HEAD)
            dq = nn(probs[h].astype(BF16), keys()).astype(BF16)
            gq[:, core, y, :, cols] = dq.reshape(CHUNKS, 16, HEAD)
            return carry

        lax.fori_loop(part * heads // 2, (part + 1) * heads // 2, body, 0)

    def put_dkv():
        for lo, src in ((0, dkt), (HEAD, dvt)):
            for n in range(CHUNKS):
                block = src[:, n * 128 : (n + 1) * 128].T.reshape(2, 4, 16, HEAD)
                for c in range(2):
                    pd[c, n, :, :, lo : lo + HEAD] = block[c]

    def grad_w_out(part):
        size = hn // 4
        rows = slice(part * size, (part + 1) * size)

        def body(m, carry):
            cols = pl.ds(pl.multiple_of(m * 1024, 1024), 1024)
            left = att[:, :, :, :, rows].reshape(1024, size)
            wo[rows, cols] = tn(left, grd[:, :, :, :, cols].reshape(1024, 1024)).astype(BF16)
            return carry

        lax.fori_loop(0, width // 1024, body, 0)
        copy = pltpu.make_async_copy(wo.at[rows], gwo.at[rows], out_sem.at[4 + part])
        copy.start()
        leaving.append(copy)

    def grad_w_in(part):
        size = width // 4
        rows = slice(part * size, (part + 1) * size)

        def body(m, carry):
            cols = pl.ds(pl.multiple_of(m * 512, 512), 512)
            left = tok[:, :, :, :, rows].reshape(1024, size)
            wq[rows, cols] = tn(left, gq[:, :, :, :, cols].reshape(1024, 512)).astype(BF16)
            return carry

        lax.fori_loop(0, hn // 512, body, 0)
        left = tok[:, :, :, :, rows].reshape(1024, size)
        wkv[:, rows] = tn(gkv[...].reshape(1024, 128), left).astype(BF16)
        moves = [(wq.at[rows], gwq.at[rows])]
        if part == 3:
            moves += [(wkv.at[0:64], gwk), (wkv.at[64:128], gwv)]
        for n, (src, dst) in enumerate(moves):
            copy = pltpu.make_async_copy(src, dst, out_sem.at[8 + part + n])
            copy.start()
            leaving.append(copy)

    is_low = jnp.full((128, 128), odd, jnp.int32) == 0

    def wait_local(copies):
        for copy in copies:
            copy.wait()
            leaving[:] = [c for c in leaving if c is not copy]

    def join_start():
        cp.start(("kv",), kvp, kvo, at_partner)

    def join_end():
        cp.arrived(("kv",))
        mine, other = kvp[...].reshape(128, 128), kvo[...].reshape(128, 128)
        low = jnp.where(is_low, mine, other)
        high = jnp.where(is_low, other, mine)
        joined = jnp.concatenate([low[:, :64], high[:, :64], low[:, 64:], high[:, 64:]], axis=1)
        kv[:, core, y] = joined.reshape(CHUNKS, 16, 2 * HEAD)

    def split_start():
        rs_wait("d", 0)
        for n in range(CHUNKS):
            dsum[n] = rs_value(xd, r2d, n)
        total = dsum[...].reshape(128, 2 * HEAD)
        lower = jnp.concatenate([total[:, 0:64], total[:, 128:192]], axis=1)
        upper = jnp.concatenate([total[:, 64:128], total[:, 192:256]], axis=1)
        dout[...] = jnp.where(is_low, upper, lower).astype(BF16)
        cp.start(("pair",), dout, dback, at_partner)
        dkeep[...] = jnp.where(is_low, lower, upper)

    def split_end():
        cp.arrived(("pair",))
        kept = (dkeep[...] + dback[...].astype(F32)).astype(BF16)
        gkv[:, core, y] = kept.reshape(CHUNKS, 16, 128)

    work = [
        (ag1, "t", tokens, tok),
        (ag1, "g", grad_out, grd),
        (wait_local, own_copies[0]),
        (wait_local, own_copies[1]),
        (ag1b, "t", tok),
        (ag1b, "g", grd),
        (ag2, "t", tok),
        (wait_local, loads[0:6]),
        (project_kv, 0),
        (project, 0),
        (rs_core, "t", pt, xt, 0, 2),
        (wait_local, loads[6:]),
        (make_mask,),
        (rs_y1, "t", pt, xt, r1t, 0, 2),
        (ag2b, "t", tok),
        (ag2, "g", grd),
        (project, 1),
        (rs_core, "t", pt, xt, 2, 2),
        (rs_y2, "t", xt, r1t, r2t, 0, 2),
        (project_kv, 1),
        (project_grad, 0),
        (rs_core, "g", pg, xg, 0, 2),
        (rs_y1, "t", pt, xt, r1t, 2, 2),
        (ag2_end, "t"),
        (project, 2),
        (rs_y1_low, "g", pg, xg, lowg, r1g, 0, 2),
        (fin_tokens, 0, 2),
        (project_kv, 2),
        (rs_core, "v", pv, xv, 0, 6),
        (rs_core, "t", pt, xt, 4, 2),
        (rs_y2, "t", xt, r1t, r2t, 2, 2),
        (rs_y1, "v", pv, xv, r1v, 0, 6),
        (rs_y2_low, "g", xg, lowg, r1g, r2g, 0, 2),
        (rs_y1, "t", pt, xt, r1t, 4, 2),
        (ag_end, "t"),
        (project_kv, 3),
        (rs_core, "v", pv, xv, 6, 2),
        (project, 3),
        (rs_core, "t", pt, xt, 6, 2),
        (fin_tokens, 2, 2),
        (rs_y1, "v", pv, xv, r1v, 6, 2),
        (rs_y2, "v", xv, r1v, r2v, 0, 6),
        (fin_grads, 0, 2),
        (rs_y1, "t", pt, xt, r1t, 6, 2),
        (ag2b, "g", grd),
        (project_grad, 1),
        (rs_y2, "v", xv, r1v, r2v, 6, 2),
        (rs_core, "g", pg, xg, 2, 2),
        (rs_y2, "t", xt, r1t, r2t, 4, 2),
        (fin_kv, 0, 6),
        (rs_y2, "t", xt, r1t, r2t, 6, 2),
        (fin_kv, 6, 2),
        (join_start,),
        (rs_y1_low, "g", pg, xg, lowg, r1g, 2, 2),
        (ag2_end, "g"),
        (project_grad, 2),
        (rs_core, "g", pg, xg, 4, 2),
        (fin_tokens, 4, 2),
        (join_end,),
        (agr1, "k", kv, None),
        (rs_y1_low, "g", pg, xg, lowg, r1g, 4, 2),
        (fin_tokens, 6, 2),
        (rs_y2_low, "g", xg, lowg, r1g, r2g, 2, 2),
        (ag_end, "g"),
        (project_grad, 3),
        (rs_core, "g", pg, xg, 6, 2),
        (agr2, "k", kv, None),
        (rs_y2_low, "g", xg, lowg, r1g, r2g, 4, 2),
        (fin_grads, 2, 2),
        (rs_y1_low, "g", pg, xg, lowg, r1g, 6, 2),
        (agr3, "k", kv, None),
        (fin_grads, 4, 2),
        (agr_end, "k"),
        (attend, 1),
        (rs_y2_low, "g", xg, lowg, r1g, r2g, 6, 2),
        (attend, 0),
        (agr1, "o0", att, 0),
        (attend, 3),
        (attend, 2),
        (agr1, "o1", att, 1),
        (fin_grads, 6, 2),
        (attend_back, 0),
        (attend_back, 1),
        (agr2, "o0", att, 0),
        (attend_back, 2),
        (attend_back, 3),
        (agr2, "o1", att, 1),
        (put_dkv,),
        (grad_query, 0),
        (agr1, "q0", gq, 0),
        (agr3, "o0", att, 0),
        (rs_core, "d", pd, xd, 0, 8),
        (grad_query, 1),
        (agr1, "q1", gq, 1),
        (agr_end, "o0"),
        (agr3, "o1", att, 1),
        (rs_y1, "d", pd, xd, r1d, 0, 8),
        (agr_end, "o1"),
        (rsc_far, "m", make_mixed, f1.at[0], 0),
        (rsc_far, "m", make_mixed, f1.at[0], 1),
        (rsc_near, "m", make_mixed, f1.at[0], f2.at[0], False, 1),
        (agr2, "q0", gq, 0),
        (rsc_own, make_mixed, 1),
        (rsc_near, "m", make_mixed, f1.at[0], f2.at[0], False, 0),
        (agr2, "q1", gq, 1),
        (rsc_own, make_mixed, 0),
        (rs_y2, "d", xd, r1d, r2d, 0, 8),
        (rsc_near, "m", make_mixed, f1.at[0], f2.at[0], True, 0),
        (agr3, "q0", gq, 0),
        (agr3, "q1", gq, 1),
        (rsc_near, "m", make_mixed, f1.at[0], f2.at[0], True, 1),
        (grad_w_out, 0),
        (split_start,),
        (agr_end, "q1"),
        (grad_w_out, 3),
        (grad_w_out, 1),
        (split_end,),
        (spread, "w", gkv),
        (grad_w_out, 2),
        (rsc_second, "m", f2.at[0], n1.at[0], 0),
        (agr_end, "q0"),
        (rsc_second, "m", f2.at[0], n1.at[0], 1),
        (rsc_third, "m", n1.at[0], n2.at[0], 0),
        (spread_end, "w"),
        (rsc_far, "x", make_gtokens, f1.at[1], 0),
        (rsc_third, "m", n1.at[0], n2.at[0], 1),
        (rsc_far, "x", make_gtokens, f1.at[1], 1),
        (rsc_near, "x", make_gtokens, f1.at[1], f2.at[1], False, 1),
        (rsc_last, "m", n2.at[0], mixed, 0, 0),
        (rsc_near, "x", make_gtokens, f1.at[1], f2.at[1], False, 0),
        (rsc_near, "x", make_gtokens, f1.at[1], f2.at[1], True, 0),
        (rsc_last, "m", n2.at[0], mixed, 0, 1),
        (rsc_own, make_gtokens, 1),
        (rsc_own, make_gtokens, 0),
        (rsc_near, "x", make_gtokens, f1.at[1], f2.at[1], True, 1),
        (grad_w_in, 2),
        (grad_w_in, 1),
        (grad_w_in, 0),
        (grad_w_in, 3),
        (rsc_second, "x", f2.at[1], n1.at[1], 0),
        (rsc_second, "x", f2.at[1], n1.at[1], 1),
        (rsc_third, "x", n1.at[1], n2.at[1], 0),
        (rsc_third, "x", n1.at[1], n2.at[1], 1),
        (rsc_last, "x", n2.at[1], gtokens, 1, 0),
        (rsc_last, "x", n2.at[1], gtokens, 1, 1),
    ]
    for step in work[:STOP]:
        step[0](*step[1:])
    wait_local(list(leaving))
    cp.finish()


def hand_over(arrays):
    count = len(arrays)
    pieces = [max(1, a.size // 2**18) for a in arrays]
    total = sum(pieces)

    def body(*refs):
        sources, results, held = refs[:count], refs[count : 2 * count], refs[2 * count : 3 * count]
        came, went = refs[-2:]
        moves = []
        for n in range(count):
            rows = arrays[n].shape[0] // pieces[n]
            for k in range(pieces[n]):
                at, m = pl.ds(k * rows, rows), len(moves)
                moves.append(
                    (
                        pltpu.make_async_copy(sources[n].at[at], held[n].at[at], came.at[m]),
                        pltpu.make_async_copy(held[n].at[at], results[n].at[at], went.at[m]),
                    )
                )
        for come, _ in moves:
            come.start()
        for come, go in moves:
            come.wait()
            go.start()
        for _, go in moves:
            go.wait()

    anywhere = pl.BlockSpec(memory_space=pl.ANY)
    return pl.pallas_call(
        body,
        out_shape=tuple(jax.ShapeDtypeStruct(a.shape, a.dtype) for a in arrays),
        in_specs=[anywhere] * count,
        out_specs=(anywhere,) * count,
        scratch_shapes=[
            *(pltpu.VMEM(a.shape, a.dtype) for a in arrays),
            pltpu.SemaphoreType.DMA((total,)),
            pltpu.SemaphoreType.DMA((total,)),
        ],
        compiler_params=pltpu.CompilerParams(vmem_limit_bytes=VMEM_LIMIT),
    )(*arrays)


def shards(tokens, segment_ids, w_query, w_key, value_weight, w_out, grad_out):
    width = tokens.shape[1]
    hn = w_query.shape[1]
    heads = hn // HEAD
    def vm(shape, dtype=BF16):
        return pltpu.VMEM(shape, dtype)

    def rs_scratch(n):
        return [
            vm((2, CHUNKS, 4, 16, n), F32),
            vm((CHUNKS, 4, 16, n), F32),
            vm((2, CHUNKS, 8, n), F32),
            vm((2, CHUNKS, 16, n), F32),
        ]

    scratch = [
        vm((2, 4, 4, 32, width)),
        vm((2, 4, 4, 32, width)),
        vm((width, hn)),
        vm((128, width)),
        vm((hn, width)),
        *rs_scratch(hn),
        *rs_scratch(128),
        vm((2, CHUNKS, 4, 16, hn), F32),
        vm((CHUNKS, 4, 16, hn), F32),
        vm((CHUNKS, 4, 16, hn)),
        vm((2, CHUNKS, 16, hn // 2)),
        vm((2, CHUNKS, 16, hn)),
        *rs_scratch(2 * HEAD),
        vm((CHUNKS, 16, hn)),
        vm((CHUNKS, 16, 128)),
        vm((CHUNKS, 16, 128)),
        vm((CHUNKS, 16, hn)),
        vm((CHUNKS, 2, 4, 16, 2 * HEAD)),
        vm((128, 1024), jnp.int32),
        vm((heads, 128, 1024), F32),
        vm((HEAD, 1024), F32),
        vm((HEAD, 1024), F32),
        vm((CHUNKS, 16, 2 * HEAD), F32),
        vm((128, 128)),
        vm((128, 128)),
        vm((128, 128), F32),
        vm((CHUNKS, 2, 4, 16, hn)),
        vm((CHUNKS, 2, 4, 16, hn)),
        vm((CHUNKS, 2, 4, 16, 128)),
        vm((2, 4, 32, width)),
        vm((2, 2, 4, 32, width)),
        vm((2, 4, 32, width), F32),
        vm((2, 2, 2, 2, 32, width)),
        vm((2, 2, 2, 4, 32, width)),
        vm((2, 2, 2, 16, width)),
        vm((2, 2, 2, 32, width)),
        vm((2, 32, width)),
        vm((2, 2, 32, width)),
        vm((2, 2, 32, width)),
        pltpu.SemaphoreType.DMA((SEMS,)),
        pltpu.SemaphoreType.DMA((SEMS,)),
        pltpu.SemaphoreType.DMA((16,)),
        pltpu.SemaphoreType.DMA((24,)),
    ]
    anywhere = pl.BlockSpec(memory_space=pl.ANY)
    inside = pl.BlockSpec(memory_space=pltpu.VMEM)
    shape = jax.ShapeDtypeStruct
    made = pl.pallas_call(
        kernel,
        out_shape=(
            shape((64, width), BF16),
            shape((64, width), BF16),
            shape((width, hn), BF16),
            shape((64, width), BF16),
            shape((64, width), BF16),
            shape((hn, width), BF16),
        ),
        in_specs=[anywhere] * 6 + [inside],
        out_specs=(anywhere,) * 6,
        scratch_shapes=scratch,
        compiler_params=pltpu.CompilerParams(
            collective_id=0, has_side_effects=True, vmem_limit_bytes=VMEM_LIMIT
        ),
    )(
        tokens, grad_out, w_query, w_key.T, value_weight.T, w_out, segment_ids.reshape(8, 128)
    )
    mixed, gtokens, gwq, gwk, gwv, gwo = hand_over(made)
    return mixed, gtokens, gwq, gwk.T, gwv.T, gwo


def solution(mesh):
    placed = (
        P("col", "row"),
        P(),
        P("row", "col"),
        P("row", "col"),
        P("row", "col"),
        P("col", "row"),
        P("col", "row"),
    )
    return jax.shard_map(
        shards,
        mesh=mesh,
        in_specs=placed,
        out_specs=(
            P("col", "row"),
            P("col", "row"),
            P("row", "col"),
            P("row", "col"),
            P("row", "col"),
            P("col", "row"),
        ),
        check_vma=False,
    )
```

```python
import jax
import jax.numpy as jnp
from jax import lax
from jax.experimental import pallas as pl
from jax.experimental.pallas import tpu as pltpu
from jax.sharding import PartitionSpec as P

HEAD = 128
CHUNKS = 8
TILE = 256
MESH = pl.DeviceIdType.MESH
F32 = jnp.float32
BF16 = jnp.bfloat16


def nn(left, right):
    return jnp.dot(left, right, preferred_element_type=F32)


def nt(left, right):
    return lax.dot_general(left, right, (((1,), (1,)), ((), ())), preferred_element_type=F32)


def tn(left, right):
    return lax.dot_general(left, right, (((0,), (0,)), ((), ())), preferred_element_type=F32)


def ring(value, step):
    return lax.rem(value + (step + 4), 4)


class Copies:
    def __init__(self, send, recv):
        self.send, self.recv = send, recv
        self.made = {}
        self.sent = set()
        self.here = set()

    def start(self, key, src, dst, device):
        index = len(self.made)
        copy = pltpu.make_async_remote_copy(
            src_ref=src,
            dst_ref=dst,
            send_sem=self.send.at[index],
            recv_sem=self.recv.at[index],
            device_id=device,
            device_id_type=MESH,
        )
        copy.start()
        self.made[key] = copy

    def arrived(self, *keys):
        for key in keys:
            if key not in self.here:
                self.made[key].wait_recv()
                self.here.add(key)

    def left(self, *keys):
        for key in keys:
            if key not in self.sent:
                self.made[key].wait_send()
                self.sent.add(key)

    def finish(self):
        self.arrived(*list(self.made))
        self.left(*list(self.made))


SEMS = 300
STOP = None
VMEM_LIMIT = 64 * 2**20


def kernel(
    tokens, grad_out, wq_in, wk_in, wv_in, wo_in, segments,
    mixed, gtokens, gwq, gwk, gwv, gwo,
    tok, grd, wq, wkv, wo,
    pt, xt, lowt, r1t, r2t, pv, xv, r1v, r2v, rv, pg, xg, lowg, r1g, r2g, pd, xd, lowd, r1d, r2d,
    qr, kvp, kvo, gh, kv, mask, probs, dkt, dvt, dsum, dout, dback, dkeep,
    att, gq, gkv,
    stfar, stnear, own, f1, f2, n1, n2, pfar, pnear, outst,
    send, recv, local, out_sem,
):
    row, col = lax.axis_index("row"), lax.axis_index("col")
    y, core = row // 2, lax.rem(row, 2)
    x, z = col // 4, lax.rem(col, 4)
    width = tok.shape[-1]
    heads = qr.shape[-1] // HEAD
    hn = heads * HEAD
    scale = HEAD ** (-0.5)

    def at_x(step):
        return {"col": ring(x, step) * 4 + z}

    def at_z(step):
        return {"col": x * 4 + ring(z, step)}

    def at_y(step):
        return {"row": ring(y, step) * 2 + core}

    at_core = {"row": y * 2 + (1 - core)}
    odd = lax.rem(z, 2)
    at_partner = {"col": x * 4 + (z + 1 - 2 * odd)}

    loads = []

    def load(src, dst):
        loads.append(pltpu.make_async_copy(src, dst, local.at[len(loads)]))

    for n in range(4):
        part = slice(n * width // 4, (n + 1) * width // 4)
        load(wq_in.at[part], wq.at[part])
    load(wk_in, wkv.at[0:64])
    load(wv_in, wkv.at[64:128])
    for n in range(4):
        part = slice(n * hn // 4, (n + 1) * hn // 4)
        load(wo_in.at[part], wo.at[part])
    leaving = []
    half = 32
    own_copies = []
    for n, (src, buf) in enumerate(((tokens, tok), (grad_out, grd))):
        own_copies.append(
            [
                pltpu.make_async_copy(src.at[0:half], buf.at[0, z, x], local.at[10 + 2 * n]),
                pltpu.make_async_copy(src.at[half:], buf.at[1, x, z], local.at[11 + 2 * n]),
            ]
        )
    for pair in own_copies:
        for copy in pair:
            copy.start()
            leaving.append(copy)
    for copy in loads:
        copy.start()
        leaving.append(copy)

    barrier = pltpu.get_barrier_semaphore()
    row_places = [(1 - core, y)] + [(c, ring(y, d)) for d in (1, -1, 2) for c in (core, 1 - core)]
    row_peers = [{"row": t * 2 + c} for c, t in row_places]
    peers = [at_x(1), at_x(-1), at_z(1), at_z(-1)] + row_peers
    for device in peers:
        pl.semaphore_signal(barrier, inc=1, device_id=device, device_id_type=MESH)
    pl.semaphore_wait(barrier, len(peers))

    cp = Copies(send, recv)

    def axes(h):
        return ((at_x, x), (at_z, z)) if h == 0 else ((at_z, z), (at_x, x))

    def ag1(name, src, buf):
        for h in range(2):
            (first, f), (_, s) = axes(h)
            for d in (1, -1):
                mine = src.at[h * half : (h + 1) * half]
                cp.start((name, 1, h, d), mine, buf.at[h, s, f], first(d))
        for h in range(2):
            (_, f), (second, s) = axes(h)
            for d in (1, -1):
                mine = src.at[h * half : (h + 1) * half]
                cp.start((name, 3, h, d, 0), mine, buf.at[h, s, f], second(d))

    def ag_second(name, buf, h, k):
        (_, f), (second, s) = axes(h)
        for d in (1, -1):
            part = buf.at[h, s, ring(f, k)]
            cp.start((name, 3, h, d, k), part, part, second(d))

    def ag1b(name, buf):
        for h in range(2):
            (first, f), (_, s) = axes(h)
            cp.arrived((name, 1, h, 1), (name, 1, h, -1))
            for d, lo in ((1, 0), (-1, 16)):
                part = buf.at[h, s, ring(f, -d), lo : lo + 16]
                cp.start((name, 2, h, d), part, part, first(d))
        for k in (1, -1):
            for h in range(2):
                ag_second(name, buf, h, k)

    def ag2(name, buf):
        for h in range(2):
            cp.arrived((name, 2, h, 1), (name, 2, h, -1))
            ag_second(name, buf, h, 2)

    def ag_on(name, buf, d, k):
        for h in range(2):
            (_, f), (second, s) = axes(h)
            cp.arrived((name, 3, h, d, k))
            part = buf.at[h, ring(s, -d), ring(f, k)]
            cp.start((name, 4, h, d, k), part, part, second(d))

    def ag2b(name, buf):
        ag_on(name, buf, 1, 0)
        ag_on(name, buf, 1, 1)
        ag_on(name, buf, -1, -1)

    def ag2c(name, buf):
        ag_on(name, buf, -1, 2)

    def ag2_end(name):
        for h in range(2):
            cp.arrived(*[(name, 3, h, d, k) for d in (1, -1) for k in (0, 1, -1, 2)])

    def ag_end(name):
        for h in range(2):
            cp.arrived(*[(name, 4, h, 1, k) for k in (0, 1)])
            cp.arrived(*[(name, 4, h, -1, k) for k in (-1, 2)])

    steps = ((0, 0), (-1, 1), (1, -1), (2, 2))
    pairs = [(ring(z, s), ring(x, s)) for s in (0, 1, -1, 2)]

    def load_pair(buf, p):
        parts = []
        for h, at in enumerate((z, x)):
            for c in range(2):
                part = buf[h, ring(at, steps[p][c]), 2 * c : 2 * c + 2]
                parts.append(part.reshape(64, width))
        return jnp.concatenate(parts, axis=0)

    def put_partial(dst, p, value, columns):
        size = value.shape[-1]
        five = value.reshape(2, 2, 4, 16, size)
        for h in range(2):
            for c in range(2):
                dst[c, 2 * p + h, :, :, columns] = five[h, c]

    def project(p):
        def body(n, carry):
            cols = pl.ds(pl.multiple_of(n * 512, 512), 512)
            put_partial(pt, p, nn(load_pair(tok, p), wq[:, cols]), cols)
            return carry

        lax.fori_loop(0, hn // 512, body, 0)

    def project_kv(p):
        put_partial(pv, p, nt(load_pair(tok, p), wkv[...]), pl.ds(0, 128))

    def project_grad(p):
        def body(n, carry):
            cols = pl.ds(pl.multiple_of(n * 512, 512), 512)
            put_partial(pg, p, nt(load_pair(grd, p), wo[cols, :]), cols)
            return carry

        lax.fori_loop(0, hn // 512, body, 0)

    def rs_core(name, part, held, s0, n):
        cp.start(
            (name, "c", s0), part.at[1 - core, pl.ds(s0, n)], held.at[pl.ds(s0, n)], at_core
        )

    def rs_y1(name, part, held, r1, s0, n):
        cp.arrived((name, "c", s0))
        for s in range(s0, s0 + n):
            held[s] = held[s] + part[core, s]
        for i, d in enumerate((1, -1)):
            cp.start(
                (name, "y1", s0, d),
                held.at[pl.ds(s0, n), ring(y, 2), 8 * i : 8 * i + 8],
                r1.at[i, pl.ds(s0, n)],
                at_y(d),
            )

    def rs_y2(name, held, r1, r2, s0, n):
        cp.arrived((name, "y1", s0, 1), (name, "y1", s0, -1))
        for i, d in enumerate((1, -1)):
            t = ring(y, d)
            lo = 8 * i
            for s in range(s0, s0 + n):
                held[s, t, lo : lo + 8] = held[s, t, lo : lo + 8] + r1[i, s]
            cp.start(
                (name, "y2", s0, d), held.at[pl.ds(s0, n), t], r2.at[i, pl.ds(s0, n)], at_y(d)
            )

    def rs_y1_low(name, part, held, low, r1, s0, n):
        cp.arrived((name, "c", s0))
        far = ring(y, 2)
        cut = held.shape[-1] // 2
        for s in range(s0, s0 + n):
            held[s] = held[s] + part[core, s]
            low[s, far] = held[s, far].astype(BF16)
        for i, d in enumerate((1, -1)):
            cp.start(
                (name, "y1", s0, d),
                low.at[pl.ds(s0, n), far, :, i * cut : (i + 1) * cut],
                r1.at[i, pl.ds(s0, n)],
                at_y(d),
            )

    def rs_y2_low(name, held, low, r1, r2, s0, n):
        cp.arrived((name, "y1", s0, 1), (name, "y1", s0, -1))
        cut = held.shape[-1] // 2
        for i, d in enumerate((1, -1)):
            t = ring(y, d)
            mid = slice(i * cut, (i + 1) * cut)
            rest = slice((1 - i) * cut, (2 - i) * cut)
            for s in range(s0, s0 + n):
                low[s, t, :, mid] = (held[s, t, :, mid] + r1[i, s].astype(F32)).astype(BF16)
                low[s, t, :, rest] = held[s, t, :, rest].astype(BF16)
            cp.start(
                (name, "y2", s0, d), low.at[pl.ds(s0, n), t], r2.at[i, pl.ds(s0, n)], at_y(d)
            )

    def rs_wait(name, s0):
        cp.arrived((name, "y2", s0, 1), (name, "y2", s0, -1))

    def rs_value(held, r2, s):
        return held[s, y] + r2[0, s].astype(F32) + r2[1, s].astype(F32)

    def chunk_of(slot):
        low, high = steps[slot // 2]
        step = low + (high - low) * core
        return ring(z, step) if slot % 2 == 0 else 4 + ring(x, step)

    def fin_tokens(s0, n):
        rs_wait("t", s0)
        for s in range(s0, s0 + n):
            qr[chunk_of(s)] = rs_value(xt, r2t, s).astype(BF16)

    def send_kv():
        for n, ((c, t), device) in enumerate(zip(row_places, row_peers)):
            cp.start(("v", n), pv.at[c, 6:8, t], rv.at[n], device)

    def fin_kv_late():
        cp.arrived(*[("v", n) for n in range(len(row_peers))])
        for s in range(2):
            total = pv[core, 6 + s, y]
            for n in range(len(row_peers)):
                total = total + rv[n, s]
            kvp[chunk_of(6 + s)] = total.astype(BF16)

    def fin_kv(s0, n):
        rs_wait("v", s0)
        for s in range(s0, s0 + n):
            kvp[chunk_of(s)] = rs_value(xv, r2v, s).astype(BF16)

    def fin_grads(s0, n):
        rs_wait("g", s0)
        for s in range(s0, s0 + n):
            gh[chunk_of(s)] = rs_value(xg, r2g, s).astype(BF16)

    def cut_of(buf, part):
        if part is None:
            return slice(None)
        size = buf.shape[-1] // 2
        return pl.ds(part * size, size)

    def agr1(name, buf, part):
        mine = buf.at[:, core, y, :, cut_of(buf, part)]
        for d in (1, -1):
            cp.start((name, "a", d), mine, mine, at_y(d))
        cp.start((name, "b", 0), mine, mine, at_core)

    def agr2(name, buf, part):
        cut = cut_of(buf, part)
        cp.arrived((name, "a", 1), (name, "a", -1))
        for d, lo in ((1, 0), (-1, 4)):
            block = buf.at[lo : lo + 4, core, ring(y, -d), :, cut]
            cp.start((name, "c", d), block, block, at_y(d))
        for d in (1, -1):
            block = buf.at[:, core, ring(y, -d), :, cut]
            cp.start((name, "b", d), block, block, at_core)

    def agr3(name, buf, part):
        cp.arrived((name, "c", 1), (name, "c", -1))
        block = buf.at[:, core, ring(y, 2), :, cut_of(buf, part)]
        cp.start((name, "b", 2), block, block, at_core)

    def agr_end(name):
        cp.arrived(*[(name, "b", k) for k in (0, 1, -1, 2)])

    def spread(name, buf):
        mine = buf.at[:, core, y]
        for n, device in enumerate(row_peers):
            cp.start((name, n), mine, mine, device)

    def spread_end(name):
        cp.arrived(*[(name, n) for n in range(len(row_peers))])

    def reuse(name, keys_):
        if name == "x":
            cp.left(*[("m", *key) for key in keys_])

    cw = width // 2

    def rsc_far(name, make, w1, part):
        cols = slice(part * cw, (part + 1) * cw)
        reuse(name, [("f", h, d, part) for h in range(2) for d in (1, -1)])
        v = make(
            [(0, pairs[3][0], 0), (0, pairs[3][0], 1), (1, pairs[3][1], 0), (1, pairs[3][1], 1)],
            cols,
        )
        for h in range(2):
            _, (second, _) = axes(h)
            for i, d in enumerate((1, -1)):
                stfar[h, 2 * i : 2 * i + 2, :, cols] = v[2 * h + i].astype(BF16)
                cp.start(
                    (name, "f", h, d, part),
                    stfar.at[h, 2 * i : 2 * i + 2, :, cols],
                    w1.at[h, i, :, :, cols],
                    second(d),
                )

    def rsc_near(name, make, w1, w2, dep, part):
        cols = slice(part * cw, (part + 1) * cw)
        items = []
        for h in range(2):
            for i in range(2):
                items.append((h, pairs[1 + i][h], i if dep else 1 - i))
        v = make(items, cols)
        for h in range(2):
            _, (second, _) = axes(h)
            if dep:
                cp.arrived((name, "f", h, 1, part), (name, "f", h, -1, part))
            for i, d in enumerate((1, -1)):
                reuse(name, [("n", h, d, dep, part)])
                at = 2 * i if dep else 2 - 2 * i
                value = v[2 * h + i]
                if dep:
                    value = value + w1[h, i, :, :, cols].astype(F32)
                stnear[h, i, at : at + 2, :, cols] = value.astype(BF16)
                cp.start(
                    (name, "n", h, d, dep, part),
                    stnear.at[h, i, at : at + 2, :, cols],
                    w2.at[h, i, at : at + 2, :, cols],
                    second(d),
                )

    def rsc_own(make, part):
        cols = slice(part * cw, (part + 1) * cw)
        v = make(
            [(0, pairs[0][0], 0), (0, pairs[0][0], 1), (1, pairs[0][1], 0), (1, pairs[0][1], 1)],
            cols,
        )
        for h in range(2):
            for i in range(2):
                own[h, 2 * i : 2 * i + 2, :, cols] = v[2 * h + i]

    def rsc_second(name, w2, v1, part):
        cols = slice(part * cw, (part + 1) * cw)
        for h in range(2):
            (first, f), _ = axes(h)
            cp.arrived(*[(name, "n", h, d, dep, part) for d in (1, -1) for dep in (False, True)])
            for k in (2, 1, -1, 0):
                s = ring(f, k)
                own[h, s, :, cols] = (
                    own[h, s, :, cols]
                    + w2[h, 0, s, :, cols].astype(F32)
                    + w2[h, 1, s, :, cols].astype(F32)
                )
                if k == 2:
                    reuse(name, [("p", h, 1, part), ("p", h, -1, part)])
                    pfar[h, :, cols] = own[h, s, :, cols].astype(BF16)
                    for i, d in enumerate((1, -1)):
                        lo = 16 * i
                        cp.start(
                            (name, "p", h, d, part),
                            pfar.at[h, lo : lo + 16, cols],
                            v1.at[h, i, :, cols],
                            first(d),
                        )

    def rsc_third(name, v1, v2, part):
        cols = slice(part * cw, (part + 1) * cw)
        for h in range(2):
            (first, f), _ = axes(h)
            cp.arrived((name, "p", h, 1, part), (name, "p", h, -1, part))
            reuse(name, [("q", h, 1, part), ("q", h, -1, part)])
            for i, d in enumerate((1, -1)):
                t = ring(f, d)
                mid = slice(16 * i, 16 * i + 16)
                rest = slice(16 - 16 * i, 32 - 16 * i)
                pnear[h, i, rest, cols] = own[h, t, rest, cols].astype(BF16)
                pnear[h, i, mid, cols] = (
                    own[h, t, mid, cols] + v1[h, i, :, cols].astype(F32)
                ).astype(BF16)
                cp.start(
                    (name, "q", h, d, part), pnear.at[h, i, :, cols], v2.at[h, i, :, cols], first(d)
                )

    def rsc_last(name, v2, dst, slot, part):
        cols = slice(part * cw, (part + 1) * cw)
        for h in range(2):
            (_, f), _ = axes(h)
            cp.arrived((name, "q", h, 1, part), (name, "q", h, -1, part))
            outst[slot, h, :, cols] = (
                own[h, f, :, cols]
                + v2[h, 0, :, cols].astype(F32)
                + v2[h, 1, :, cols].astype(F32)
            ).astype(BF16)
            copy = pltpu.make_async_copy(
                outst.at[slot, h, :, cols],
                dst.at[h * half : (h + 1) * half, cols],
                out_sem.at[16 + 4 * slot + 2 * part + h],
            )
            copy.start()
            leaving.append(copy)

    def rows_of(buf, items):
        return jnp.concatenate(
            [buf[4 * h + b, c].reshape(64, buf.shape[-1]) for h, b, c in items], axis=0
        )

    def make_mixed(items, cols):
        return nn(rows_of(att, items), wo[:, cols]).reshape(4, 2, 32, cw)

    def make_gtokens(items, cols):
        v = nt(rows_of(gq, items), wq[cols, :]) + nn(rows_of(gkv, items), wkv[:, cols])
        return v.reshape(4, 2, 32, cw)

    def keys():
        return kv[:, :, :, :, 0:HEAD].reshape(1024, HEAD)

    def vals():
        return kv[:, :, :, :, HEAD : 2 * HEAD].reshape(1024, HEAD)

    def place(p):
        i, s, b, h = p & 31, (p >> 5) & 3, (p >> 7) & 3, p >> 9
        xs = jnp.where(h == 0, s, b)
        zs = jnp.where(h == 0, b, s)
        return xs * 256 + zs * 64 + h * 32 + i

    def make_mask():
        seg = segments[...].astype(F32)
        seg = jnp.concatenate([seg[n : n + 1] for n in range(8)], axis=1)
        shape = (1024, 1024)
        key_place = place(lax.broadcasted_iota(jnp.int32, (1, 1024), 1))
        pick = lax.broadcasted_iota(jnp.int32, shape, 0) == key_place
        key_seg = nn(
            jnp.broadcast_to(seg, (16, 1024)).astype(BF16), pick.astype(F32).astype(BF16)
        )[0:1]
        r = lax.broadcasted_iota(jnp.int32, (128, 1), 0)
        mine = place(((r >> 4) << 7) + core * 64 + y * 16 + (r & 15))
        here = lax.broadcasted_iota(jnp.int32, (128, 1024), 1) == mine
        my_seg = jnp.sum(jnp.where(here, seg, F32(0)), axis=1, keepdims=True)
        mask[...] = ((my_seg == key_seg) & (key_place <= mine)).astype(jnp.int32)

    def attend(part):
        def body(h, carry):
            cols = pl.ds(pl.multiple_of(h * HEAD, HEAD), HEAD)
            q = qr[:, :, cols].reshape(128, HEAD)
            s = nt(q, keys()) * scale
            s = jnp.where(mask[...] > 0, s, F32(-1e30))
            e = jnp.exp(s - jnp.max(s, axis=-1, keepdims=True))
            p = e / jnp.sum(e, axis=-1, keepdims=True)
            probs[h] = p
            o = nn(p.astype(BF16), vals()).astype(BF16)
            att[:, core, y, :, cols] = o.reshape(CHUNKS, 16, HEAD)
            return carry

        lax.fori_loop(part * heads // 4, (part + 1) * heads // 4, body, 0)

    def attend_back(part):
        if part == 0:
            dkt[...] = jnp.zeros_like(dkt)
            dvt[...] = jnp.zeros_like(dvt)

        def body(h, carry):
            cols = pl.ds(pl.multiple_of(h * HEAD, HEAD), HEAD)
            q = qr[:, :, cols].reshape(128, HEAD)
            g = gh[:, :, cols].reshape(128, HEAD)
            p = probs[h]
            dp = nt(g, vals())
            inner = jnp.sum(p * dp, axis=-1, keepdims=True)
            ds = (p * (dp - inner) * scale).astype(BF16)
            probs[h] = ds.astype(F32)
            dkt[...] += nn(q.T, ds)
            dvt[...] += nn(g.T, p.astype(BF16))
            return carry

        lax.fori_loop(part * heads // 4, (part + 1) * heads // 4, body, 0)

    def grad_query(part):
        def body(h, carry):
            cols = pl.ds(pl.multiple_of(h * HEAD, HEAD), HEAD)
            dq = nn(probs[h].astype(BF16), keys()).astype(BF16)
            gq[:, core, y, :, cols] = dq.reshape(CHUNKS, 16, HEAD)
            return carry

        lax.fori_loop(part * heads // 2, (part + 1) * heads // 2, body, 0)

    def put_dkv():
        for lo, src in ((0, dkt), (HEAD, dvt)):
            for n in range(CHUNKS):
                block = src[:, n * 128 : (n + 1) * 128].T.reshape(2, 4, 16, HEAD)
                for c in range(2):
                    pd[c, n, :, :, lo : lo + HEAD] = block[c]

    def grad_w_out(part):
        size = hn // 4
        rows = slice(part * size, (part + 1) * size)

        def body(m, carry):
            cols = pl.ds(pl.multiple_of(m * 1024, 1024), 1024)
            left = att[:, :, :, :, rows].reshape(1024, size)
            wo[rows, cols] = tn(left, grd[:, :, :, :, cols].reshape(1024, 1024)).astype(BF16)
            return carry

        lax.fori_loop(0, width // 1024, body, 0)
        copy = pltpu.make_async_copy(wo.at[rows], gwo.at[rows], out_sem.at[4 + part])
        copy.start()
        leaving.append(copy)

    def grad_w_in(part):
        size = width // 4
        rows = slice(part * size, (part + 1) * size)

        def body(m, carry):
            cols = pl.ds(pl.multiple_of(m * 512, 512), 512)
            left = tok[:, :, :, :, rows].reshape(1024, size)
            wq[rows, cols] = tn(left, gq[:, :, :, :, cols].reshape(1024, 512)).astype(BF16)
            return carry

        lax.fori_loop(0, hn // 512, body, 0)
        left = tok[:, :, :, :, rows].reshape(1024, size)
        wkv[:, rows] = tn(gkv[...].reshape(1024, 128), left).astype(BF16)
        moves = [(wq.at[rows], gwq.at[rows])]
        if part == 3:
            moves += [(wkv.at[0:64], gwk), (wkv.at[64:128], gwv)]
        for n, (src, dst) in enumerate(moves):
            copy = pltpu.make_async_copy(src, dst, out_sem.at[8 + part + n])
            copy.start()
            leaving.append(copy)

    is_low = jnp.full((128, 128), odd, jnp.int32) == 0

    def wait_local(copies):
        for copy in copies:
            copy.wait()
            leaving[:] = [c for c in leaving if c is not copy]

    def join_start():
        cp.start(("kv",), kvp, kvo, at_partner)

    def join_end():
        cp.arrived(("kv",))
        mine, other = kvp[...].reshape(128, 128), kvo[...].reshape(128, 128)
        low = jnp.where(is_low, mine, other)
        high = jnp.where(is_low, other, mine)
        joined = jnp.concatenate([low[:, :64], high[:, :64], low[:, 64:], high[:, 64:]], axis=1)
        kv[:, core, y] = joined.reshape(CHUNKS, 16, 2 * HEAD)

    def split_start():
        rs_wait("d", 0)
        for n in range(CHUNKS):
            dsum[n] = rs_value(xd, r2d, n)
        total = dsum[...].reshape(128, 2 * HEAD)
        lower = jnp.concatenate([total[:, 0:64], total[:, 128:192]], axis=1)
        upper = jnp.concatenate([total[:, 64:128], total[:, 192:256]], axis=1)
        dout[...] = jnp.where(is_low, upper, lower).astype(BF16)
        cp.start(("pair",), dout, dback, at_partner)
        dkeep[...] = jnp.where(is_low, lower, upper)

    def split_end():
        cp.arrived(("pair",))
        kept = (dkeep[...] + dback[...].astype(F32)).astype(BF16)
        gkv[:, core, y] = kept.reshape(CHUNKS, 16, 128)

    work = [
        (ag1, "t", tokens, tok),
        (wait_local, own_copies[0]),
        (ag1b, "t", tok),
        (ag2, "t", tok),
        (wait_local, loads[0:6]),
        (project, 0),
        (rs_core, "t", pt, xt, 0, 2),
        (project_kv, 0),
        (wait_local, loads[6:]),
        (make_mask,),
        (rs_y1_low, "t", pt, xt, lowt, r1t, 0, 2),
        (ag2b, "t", tok),
        (rs_y2_low, "t", xt, lowt, r1t, r2t, 0, 2),
        (ag2c, "t", tok),
        (ag1, "g", grad_out, grd),
        (wait_local, own_copies[1]),
        (ag2_end, "t"),
        (project_kv, 2),
        (project_kv, 1),
        (rs_core, "v", pv, xv, 0, 6),
        (project, 2),
        (rs_core, "t", pt, xt, 4, 2),
        (project, 1),
        (rs_y1, "v", pv, xv, r1v, 0, 6),
        (fin_tokens, 0, 2),
        (rs_core, "t", pt, xt, 2, 2),
        (ag_end, "t"),
        (project_kv, 3),
        (send_kv,),
        (project, 3),
        (rs_core, "t", pt, xt, 6, 2),
        (rs_y1_low, "t", pt, xt, lowt, r1t, 2, 2),
        (ag1b, "g", grd),
        (rs_y1_low, "t", pt, xt, lowt, r1t, 4, 2),
        (rs_y2, "v", xv, r1v, r2v, 0, 6),
        (rs_y1_low, "t", pt, xt, lowt, r1t, 6, 2),
        (fin_kv_late,),
        (rs_y2_low, "t", xt, lowt, r1t, r2t, 2, 2),
        (rs_y2_low, "t", xt, lowt, r1t, r2t, 4, 2),
        (ag2, "g", grd),
        (project_grad, 0),
        (rs_core, "g", pg, xg, 0, 2),
        (rs_y2_low, "t", xt, lowt, r1t, r2t, 6, 2),
        (fin_kv, 0, 6),
        (join_start,),
        (fin_tokens, 2, 2),
        (fin_tokens, 4, 2),
        (rs_y1_low, "g", pg, xg, lowg, r1g, 0, 2),
        (join_end,),
        (ag2b, "g", grd),
        (fin_tokens, 6, 2),
        (agr1, "k", kv, None),
        (rs_y2_low, "g", xg, lowg, r1g, r2g, 0, 2),
        (ag2_end, "g"),
        (ag2c, "g", grd),
        (project_grad, 1),
        (rs_core, "g", pg, xg, 2, 2),
        (agr2, "k", kv, None),
        (project_grad, 2),
        (fin_grads, 0, 2),
        (rs_core, "g", pg, xg, 4, 2),
        (rs_y1_low, "g", pg, xg, lowg, r1g, 2, 2),
        (agr3, "k", kv, None),
        (ag_end, "g"),
        (project_grad, 3),
        (rs_y1_low, "g", pg, xg, lowg, r1g, 4, 2),
        (agr_end, "k"),
        (rs_core, "g", pg, xg, 6, 2),
        (attend, 0),
        (rs_y2_low, "g", xg, lowg, r1g, r2g, 2, 2),
        (attend, 2),
        (rs_y2_low, "g", xg, lowg, r1g, r2g, 4, 2),
        (rs_y1_low, "g", pg, xg, lowg, r1g, 6, 2),
        (attend, 3),
        (agr1, "o1", att, 1),
        (attend, 1),
        (fin_grads, 2, 2),
        (agr1, "o0", att, 0),
        (fin_grads, 4, 2),
        (rs_y2_low, "g", xg, lowg, r1g, r2g, 6, 2),
        (agr2, "o1", att, 1),
        (agr2, "o0", att, 0),
        (fin_grads, 6, 2),
        (attend_back, 0),
        (agr3, "o1", att, 1),
        (attend_back, 1),
        (agr3, "o0", att, 0),
        (attend_back, 2),
        (agr_end, "o1"),
        (attend_back, 3),
        (put_dkv,),
        (rs_core, "d", pd, xd, 0, 8),
        (agr_end, "o0"),
        (rsc_far, "m", make_mixed, f1.at[0], 1),
        (grad_query, 0),
        (rsc_far, "m", make_mixed, f1.at[0], 0),
        (rsc_near, "m", make_mixed, f1.at[0], f2.at[0], False, 0),
        (rs_y1_low, "d", pd, xd, lowd, r1d, 0, 8),
        (rsc_own, make_mixed, 0),
        (agr1, "q0", gq, 0),
        (rsc_near, "m", make_mixed, f1.at[0], f2.at[0], False, 1),
        (rsc_own, make_mixed, 1),
        (grad_query, 1),
        (rs_y2_low, "d", xd, lowd, r1d, r2d, 0, 8),
        (rsc_near, "m", make_mixed, f1.at[0], f2.at[0], True, 1),
        (agr1, "q1", gq, 1),
        (rsc_near, "m", make_mixed, f1.at[0], f2.at[0], True, 0),
        (agr2, "q0", gq, 0),
        (grad_w_out, 0),
        (split_start,),
        (grad_w_out, 1),
        (agr2, "q1", gq, 1),
        (split_end,),
        (spread, "w", gkv),
        (agr3, "q0", gq, 0),
        (grad_w_out, 3),
        (rsc_second, "m", f2.at[0], n1.at[0], 1),
        (agr3, "q1", gq, 1),
        (agr_end, "q0"),
        (grad_w_out, 2),
        (rsc_second, "m", f2.at[0], n1.at[0], 0),
        (agr_end, "q1"),
        (rsc_third, "m", n1.at[0], n2.at[0], 1),
        (spread_end, "w"),
        (rsc_far, "x", make_gtokens, f1.at[1], 1),
        (rsc_far, "x", make_gtokens, f1.at[1], 0),
        (rsc_third, "m", n1.at[0], n2.at[0], 0),
        (rsc_near, "x", make_gtokens, f1.at[1], f2.at[1], False, 1),
        (rsc_near, "x", make_gtokens, f1.at[1], f2.at[1], False, 0),
        (rsc_last, "m", n2.at[0], mixed, 0, 1),
        (rsc_near, "x", make_gtokens, f1.at[1], f2.at[1], True, 1),
        (rsc_near, "x", make_gtokens, f1.at[1], f2.at[1], True, 0),
        (rsc_last, "m", n2.at[0], mixed, 0, 0),
        (rsc_own, make_gtokens, 1),
        (rsc_own, make_gtokens, 0),
        (grad_w_in, 2),
        (grad_w_in, 1),
        (grad_w_in, 0),
        (rsc_second, "x", f2.at[1], n1.at[1], 1),
        (grad_w_in, 3),
        (rsc_second, "x", f2.at[1], n1.at[1], 0),
        (rsc_third, "x", n1.at[1], n2.at[1], 1),
        (rsc_third, "x", n1.at[1], n2.at[1], 0),
        (rsc_last, "x", n2.at[1], gtokens, 1, 1),
        (rsc_last, "x", n2.at[1], gtokens, 1, 0),
    ]
    for step in work[:STOP]:
        step[0](*step[1:])
    wait_local(list(leaving))
    cp.finish()


def hand_over(arrays):
    count = len(arrays)
    pieces = [max(1, a.size // 2**18) for a in arrays]
    total = sum(pieces)

    def body(*refs):
        sources, results, held = refs[:count], refs[count : 2 * count], refs[2 * count : 3 * count]
        came, went = refs[-2:]
        moves = []
        for n in range(count):
            rows = arrays[n].shape[0] // pieces[n]
            for k in range(pieces[n]):
                at, m = pl.ds(k * rows, rows), len(moves)
                moves.append(
                    (
                        pltpu.make_async_copy(sources[n].at[at], held[n].at[at], came.at[m]),
                        pltpu.make_async_copy(held[n].at[at], results[n].at[at], went.at[m]),
                    )
                )
        for come, _ in moves:
            come.start()
        for come, go in moves:
            come.wait()
            go.start()
        for _, go in moves:
            go.wait()

    anywhere = pl.BlockSpec(memory_space=pl.ANY)
    return pl.pallas_call(
        body,
        out_shape=tuple(jax.ShapeDtypeStruct(a.shape, a.dtype) for a in arrays),
        in_specs=[anywhere] * count,
        out_specs=(anywhere,) * count,
        scratch_shapes=[
            *(pltpu.VMEM(a.shape, a.dtype) for a in arrays),
            pltpu.SemaphoreType.DMA((total,)),
            pltpu.SemaphoreType.DMA((total,)),
        ],
        compiler_params=pltpu.CompilerParams(vmem_limit_bytes=VMEM_LIMIT),
    )(*arrays)


def shards(tokens, segment_ids, w_query, w_key, value_weight, w_out, grad_out):
    width = tokens.shape[1]
    hn = w_query.shape[1]
    heads = hn // HEAD
    def vm(shape, dtype=BF16):
        return pltpu.VMEM(shape, dtype)

    def rs_scratch(n):
        return [
            vm((2, CHUNKS, 4, 16, n), F32),
            vm((CHUNKS, 4, 16, n), F32),
            vm((2, CHUNKS, 8, n), F32),
            vm((2, CHUNKS, 16, n), F32),
        ]

    scratch = [
        vm((2, 4, 4, 32, width)),
        vm((2, 4, 4, 32, width)),
        vm((width, hn)),
        vm((128, width)),
        vm((hn, width)),
        vm((2, CHUNKS, 4, 16, hn), F32),
        vm((CHUNKS, 4, 16, hn), F32),
        vm((CHUNKS, 4, 16, hn)),
        vm((2, CHUNKS, 16, hn // 2)),
        vm((2, CHUNKS, 16, hn)),
        *rs_scratch(128),
        vm((7, 2, 16, 128), F32),
        vm((2, CHUNKS, 4, 16, hn), F32),
        vm((CHUNKS, 4, 16, hn), F32),
        vm((CHUNKS, 4, 16, hn)),
        vm((2, CHUNKS, 16, hn // 2)),
        vm((2, CHUNKS, 16, hn)),
        vm((2, CHUNKS, 4, 16, 2 * HEAD), F32),
        vm((CHUNKS, 4, 16, 2 * HEAD), F32),
        vm((CHUNKS, 4, 16, 2 * HEAD)),
        vm((2, CHUNKS, 16, HEAD)),
        vm((2, CHUNKS, 16, 2 * HEAD)),
        vm((CHUNKS, 16, hn)),
        vm((CHUNKS, 16, 128)),
        vm((CHUNKS, 16, 128)),
        vm((CHUNKS, 16, hn)),
        vm((CHUNKS, 2, 4, 16, 2 * HEAD)),
        vm((128, 1024), jnp.int32),
        vm((heads, 128, 1024), F32),
        vm((HEAD, 1024), F32),
        vm((HEAD, 1024), F32),
        vm((CHUNKS, 16, 2 * HEAD), F32),
        vm((128, 128)),
        vm((128, 128)),
        vm((128, 128), F32),
        vm((CHUNKS, 2, 4, 16, hn)),
        vm((CHUNKS, 2, 4, 16, hn)),
        vm((CHUNKS, 2, 4, 16, 128)),
        vm((2, 4, 32, width)),
        vm((2, 2, 4, 32, width)),
        vm((2, 4, 32, width), F32),
        vm((2, 2, 2, 2, 32, width)),
        vm((2, 2, 2, 4, 32, width)),
        vm((2, 2, 2, 16, width)),
        vm((2, 2, 2, 32, width)),
        vm((2, 32, width)),
        vm((2, 2, 32, width)),
        vm((2, 2, 32, width)),
        pltpu.SemaphoreType.DMA((SEMS,)),
        pltpu.SemaphoreType.DMA((SEMS,)),
        pltpu.SemaphoreType.DMA((16,)),
        pltpu.SemaphoreType.DMA((24,)),
    ]
    anywhere = pl.BlockSpec(memory_space=pl.ANY)
    inside = pl.BlockSpec(memory_space=pltpu.VMEM)
    shape = jax.ShapeDtypeStruct
    made = pl.pallas_call(
        kernel,
        out_shape=(
            shape((64, width), BF16),
            shape((64, width), BF16),
            shape((width, hn), BF16),
            shape((64, width), BF16),
            shape((64, width), BF16),
            shape((hn, width), BF16),
        ),
        in_specs=[anywhere] * 6 + [inside],
        out_specs=(anywhere,) * 6,
        scratch_shapes=scratch,
        compiler_params=pltpu.CompilerParams(
            collective_id=0, has_side_effects=True, vmem_limit_bytes=VMEM_LIMIT
        ),
    )(
        tokens, grad_out, w_query, w_key.T, value_weight.T, w_out, segment_ids.reshape(8, 128)
    )
    mixed, gtokens, gwq, gwk, gwv, gwo = hand_over(made)
    return mixed, gtokens, gwq, gwk.T, gwv.T, gwo


def solution(mesh):
    placed = (
        P("col", "row"),
        P(),
        P("row", "col"),
        P("row", "col"),
        P("row", "col"),
        P("col", "row"),
        P("col", "row"),
    )
    return jax.shard_map(
        shards,
        mesh=mesh,
        in_specs=placed,
        out_specs=(
            P("col", "row"),
            P("col", "row"),
            P("row", "col"),
            P("row", "col"),
            P("row", "col"),
            P("col", "row"),
        ),
        check_vma=False,
    )
```

```python
import jax
import jax.numpy as jnp
from jax import lax
from jax.experimental import pallas as pl
from jax.experimental.pallas import tpu as pltpu
from jax.sharding import PartitionSpec as P

HEAD = 128
CHUNKS = 8
TILE = 256
MESH = pl.DeviceIdType.MESH
F32 = jnp.float32
BF16 = jnp.bfloat16


def nn(left, right):
    return jnp.dot(left, right, preferred_element_type=F32)


def nt(left, right):
    return lax.dot_general(left, right, (((1,), (1,)), ((), ())), preferred_element_type=F32)


def tn(left, right):
    return lax.dot_general(left, right, (((0,), (0,)), ((), ())), preferred_element_type=F32)


def ring(value, step):
    return lax.rem(value + (step + 4), 4)


class Copies:
    def __init__(self, send, recv):
        self.send, self.recv = send, recv
        self.made = {}
        self.sent = set()
        self.here = set()

    def start(self, key, src, dst, device):
        index = len(self.made)
        copy = pltpu.make_async_remote_copy(
            src_ref=src,
            dst_ref=dst,
            send_sem=self.send.at[index],
            recv_sem=self.recv.at[index],
            device_id=device,
            device_id_type=MESH,
        )
        copy.start()
        self.made[key] = copy

    def arrived(self, *keys):
        for key in keys:
            if key not in self.here:
                self.made[key].wait_recv()
                self.here.add(key)

    def left(self, *keys):
        for key in keys:
            if key not in self.sent:
                self.made[key].wait_send()
                self.sent.add(key)

    def finish(self):
        self.arrived(*list(self.made))
        self.left(*list(self.made))


SEMS = 300
STOP = None
VMEM_LIMIT = 64 * 2**20


def kernel(
    tokens, grad_out, wq_in, wk_in, wv_in, wo_in, segments,
    mixed, gtokens, gwq, gwk, gwv, gwo,
    tok, grd, wq, wkv, wo,
    pt, xt, r1t, r2t, pv, xv, r1v, r2v, rv, pg, xg, lowg, r1g, r2g, pd, xd, lowd, r1d, r2d,
    qr, kvp, kvo, gh, kv, mask, probs, dkt, dvt, dsum, dout, dback, dkeep,
    att, gq, gkv,
    stfar, stnear, own, f1, f2, n1, n2, pfar, pnear, outst,
    send, recv, local, out_sem,
):
    row, col = lax.axis_index("row"), lax.axis_index("col")
    y, core = row // 2, lax.rem(row, 2)
    x, z = col // 4, lax.rem(col, 4)
    width = tok.shape[-1]
    heads = qr.shape[-1] // HEAD
    hn = heads * HEAD
    scale = HEAD ** (-0.5)

    def at_x(step):
        return {"col": ring(x, step) * 4 + z}

    def at_z(step):
        return {"col": x * 4 + ring(z, step)}

    def at_y(step):
        return {"row": ring(y, step) * 2 + core}

    at_core = {"row": y * 2 + (1 - core)}
    odd = lax.rem(z, 2)
    at_partner = {"col": x * 4 + (z + 1 - 2 * odd)}

    loads = []

    def load(src, dst):
        loads.append(pltpu.make_async_copy(src, dst, local.at[len(loads)]))

    for n in range(4):
        part = slice(n * width // 4, (n + 1) * width // 4)
        load(wq_in.at[part], wq.at[part])
    load(wk_in, wkv.at[0:64])
    load(wv_in, wkv.at[64:128])
    for n in range(4):
        part = slice(n * hn // 4, (n + 1) * hn // 4)
        load(wo_in.at[part], wo.at[part])
    leaving = []
    half = 32
    own_copies = []
    for n, (src, buf) in enumerate(((tokens, tok), (grad_out, grd))):
        own_copies.append(
            [
                pltpu.make_async_copy(src.at[0:half], buf.at[0, z, x], local.at[10 + 2 * n]),
                pltpu.make_async_copy(src.at[half:], buf.at[1, x, z], local.at[11 + 2 * n]),
            ]
        )
    for pair in own_copies:
        for copy in pair:
            copy.start()
            leaving.append(copy)

    def start_local(copies):
        for copy in copies:
            copy.start()
            leaving.append(copy)

    barrier = pltpu.get_barrier_semaphore()
    row_places = [(1 - core, y)] + [(c, ring(y, d)) for d in (1, -1, 2) for c in (core, 1 - core)]
    row_peers = [{"row": t * 2 + c} for c, t in row_places]
    peers = [at_x(1), at_x(-1), at_z(1), at_z(-1)] + row_peers
    for device in peers:
        pl.semaphore_signal(barrier, inc=1, device_id=device, device_id_type=MESH)
    pl.semaphore_wait(barrier, len(peers))

    cp = Copies(send, recv)

    def axes(h):
        return ((at_x, x), (at_z, z)) if h == 0 else ((at_z, z), (at_x, x))

    def ag1(name, src, buf):
        for h in range(2):
            (first, f), (_, s) = axes(h)
            for d in (1, -1):
                mine = src.at[h * half : (h + 1) * half]
                cp.start((name, 1, h, d), mine, buf.at[h, s, f], first(d))
        for h in range(2):
            (_, f), (second, s) = axes(h)
            for d in (1, -1):
                mine = src.at[h * half : (h + 1) * half]
                cp.start((name, 3, h, d, 0), mine, buf.at[h, s, f], second(d))

    def ag_second(name, buf, h, k):
        (_, f), (second, s) = axes(h)
        for d in (1, -1):
            part = buf.at[h, s, ring(f, k)]
            cp.start((name, 3, h, d, k), part, part, second(d))

    def ag1b(name, buf):
        for h in range(2):
            (first, f), (_, s) = axes(h)
            cp.arrived((name, 1, h, 1), (name, 1, h, -1))
            for d, lo in ((1, 0), (-1, 16)):
                part = buf.at[h, s, ring(f, -d), lo : lo + 16]
                cp.start((name, 2, h, d), part, part, first(d))
        for k in (1, -1):
            for h in range(2):
                ag_second(name, buf, h, k)

    def ag2(name, buf):
        for h in range(2):
            cp.arrived((name, 2, h, 1), (name, 2, h, -1))
            ag_second(name, buf, h, 2)

    def ag_on(name, buf, d, k):
        for h in range(2):
            (_, f), (second, s) = axes(h)
            cp.arrived((name, 3, h, d, k))
            part = buf.at[h, ring(s, -d), ring(f, k)]
            cp.start((name, 4, h, d, k), part, part, second(d))

    def ag2b(name, buf):
        ag_on(name, buf, 1, 0)
        ag_on(name, buf, 1, 1)
        ag_on(name, buf, -1, -1)

    def ag2c(name, buf):
        ag_on(name, buf, -1, 2)

    def ag2_end(name):
        for h in range(2):
            cp.arrived(*[(name, 3, h, d, k) for d in (1, -1) for k in (0, 1, -1, 2)])

    def ag_end(name):
        for h in range(2):
            cp.arrived(*[(name, 4, h, 1, k) for k in (0, 1)])
            cp.arrived(*[(name, 4, h, -1, k) for k in (-1, 2)])

    steps = ((0, 0), (-1, 1), (1, -1), (2, 2))
    pairs = [(ring(z, s), ring(x, s)) for s in (0, 1, -1, 2)]

    def load_pair(buf, p):
        parts = []
        for h, at in enumerate((z, x)):
            for c in range(2):
                part = buf[h, ring(at, steps[p][c]), 2 * c : 2 * c + 2]
                parts.append(part.reshape(64, width))
        return jnp.concatenate(parts, axis=0)

    def put_partial(dst, p, value, columns):
        size = value.shape[-1]
        five = value.reshape(2, 2, 4, 16, size)
        for h in range(2):
            for c in range(2):
                dst[c, 2 * p + h, :, :, columns] = five[h, c]

    def project(p):
        def body(n, carry):
            cols = pl.ds(pl.multiple_of(n * 512, 512), 512)
            put_partial(pt, p, nn(load_pair(tok, p), wq[:, cols]), cols)
            return carry

        lax.fori_loop(0, hn // 512, body, 0)

    def project_kv(p):
        put_partial(pv, p, nt(load_pair(tok, p), wkv[...]), pl.ds(0, 128))

    def project_grad(p):
        def body(n, carry):
            cols = pl.ds(pl.multiple_of(n * 512, 512), 512)
            put_partial(pg, p, nt(load_pair(grd, p), wo[cols, :]), cols)
            return carry

        lax.fori_loop(0, hn // 512, body, 0)

    def rs_core(name, part, held, s0, n):
        cp.start(
            (name, "c", s0), part.at[1 - core, pl.ds(s0, n)], held.at[pl.ds(s0, n)], at_core
        )

    def rs_y1(name, part, held, r1, s0, n):
        cp.arrived((name, "c", s0))
        for s in range(s0, s0 + n):
            held[s] = held[s] + part[core, s]
        for i, d in enumerate((1, -1)):
            cp.start(
                (name, "y1", s0, d),
                held.at[pl.ds(s0, n), ring(y, 2), 8 * i : 8 * i + 8],
                r1.at[i, pl.ds(s0, n)],
                at_y(d),
            )

    def rs_y2(name, held, r1, r2, s0, n):
        cp.arrived((name, "y1", s0, 1), (name, "y1", s0, -1))
        for i, d in enumerate((1, -1)):
            t = ring(y, d)
            lo = 8 * i
            for s in range(s0, s0 + n):
                held[s, t, lo : lo + 8] = held[s, t, lo : lo + 8] + r1[i, s]
            cp.start(
                (name, "y2", s0, d), held.at[pl.ds(s0, n), t], r2.at[i, pl.ds(s0, n)], at_y(d)
            )

    def rs_y1_low(name, part, held, low, r1, s0, n):
        cp.arrived((name, "c", s0))
        far = ring(y, 2)
        cut = held.shape[-1] // 2
        for s in range(s0, s0 + n):
            held[s] = held[s] + part[core, s]
            low[s, far] = held[s, far].astype(BF16)
        for i, d in enumerate((1, -1)):
            cp.start(
                (name, "y1", s0, d),
                low.at[pl.ds(s0, n), far, :, i * cut : (i + 1) * cut],
                r1.at[i, pl.ds(s0, n)],
                at_y(d),
            )

    def rs_y2_low(name, held, low, r1, r2, s0, n):
        cp.arrived((name, "y1", s0, 1), (name, "y1", s0, -1))
        cut = held.shape[-1] // 2
        for i, d in enumerate((1, -1)):
            t = ring(y, d)
            mid = slice(i * cut, (i + 1) * cut)
            rest = slice((1 - i) * cut, (2 - i) * cut)
            for s in range(s0, s0 + n):
                low[s, t, :, mid] = (held[s, t, :, mid] + r1[i, s].astype(F32)).astype(BF16)
                low[s, t, :, rest] = held[s, t, :, rest].astype(BF16)
            cp.start(
                (name, "y2", s0, d), low.at[pl.ds(s0, n), t], r2.at[i, pl.ds(s0, n)], at_y(d)
            )

    def rs_wait(name, s0):
        cp.arrived((name, "y2", s0, 1), (name, "y2", s0, -1))

    def rs_value(held, r2, s):
        return held[s, y] + r2[0, s].astype(F32) + r2[1, s].astype(F32)

    def chunk_of(slot):
        low, high = steps[slot // 2]
        step = low + (high - low) * core
        return ring(z, step) if slot % 2 == 0 else 4 + ring(x, step)

    def fin_tokens(s0, n):
        rs_wait("t", s0)
        for s in range(s0, s0 + n):
            qr[chunk_of(s)] = rs_value(xt, r2t, s).astype(BF16)

    def send_kv():
        for n, ((c, t), device) in enumerate(zip(row_places, row_peers)):
            cp.start(("v", n), pv.at[c, 6:8, t], rv.at[n], device)

    def fin_kv_late():
        cp.arrived(*[("v", n) for n in range(len(row_peers))])
        for s in range(2):
            total = pv[core, 6 + s, y]
            for n in range(len(row_peers)):
                total = total + rv[n, s]
            kvp[chunk_of(6 + s)] = total.astype(BF16)

    def fin_kv(s0, n):
        rs_wait("v", s0)
        for s in range(s0, s0 + n):
            kvp[chunk_of(s)] = rs_value(xv, r2v, s).astype(BF16)

    def fin_grads(s0, n):
        rs_wait("g", s0)
        for s in range(s0, s0 + n):
            gh[chunk_of(s)] = rs_value(xg, r2g, s).astype(BF16)

    def cut_of(buf, part):
        if part is None:
            return slice(None)
        size = buf.shape[-1] // 2
        return pl.ds(part * size, size)

    def agr1(name, buf, part):
        mine = buf.at[:, core, y, :, cut_of(buf, part)]
        for d in (1, -1):
            cp.start((name, "a", d), mine, mine, at_y(d))
        cp.start((name, "b", 0), mine, mine, at_core)

    def agr2(name, buf, part):
        cut = cut_of(buf, part)
        cp.arrived((name, "a", 1), (name, "a", -1))
        for d, lo in ((1, 0), (-1, 4)):
            block = buf.at[lo : lo + 4, core, ring(y, -d), :, cut]
            cp.start((name, "c", d), block, block, at_y(d))
        for d in (1, -1):
            block = buf.at[:, core, ring(y, -d), :, cut]
            cp.start((name, "b", d), block, block, at_core)

    def agr3(name, buf, part):
        cp.arrived((name, "c", 1), (name, "c", -1))
        block = buf.at[:, core, ring(y, 2), :, cut_of(buf, part)]
        cp.start((name, "b", 2), block, block, at_core)

    def agr_end(name):
        cp.arrived(*[(name, "b", k) for k in (0, 1, -1, 2)])

    def spread(name, buf):
        mine = buf.at[:, core, y]
        for n, device in enumerate(row_peers):
            cp.start((name, n), mine, mine, device)

    def spread_end(name):
        cp.arrived(*[(name, n) for n in range(len(row_peers))])

    def reuse(name, keys_):
        if name == "x":
            cp.left(*[("m", *key) for key in keys_])

    cw = width // 2

    def rsc_far(name, make, w1, part):
        cols = slice(part * cw, (part + 1) * cw)
        reuse(name, [("f", h, d, part) for h in range(2) for d in (1, -1)])
        v = make(
            [(0, pairs[3][0], 0), (0, pairs[3][0], 1), (1, pairs[3][1], 0), (1, pairs[3][1], 1)],
            cols,
        )
        for h in range(2):
            _, (second, _) = axes(h)
            for i, d in enumerate((1, -1)):
                stfar[h, 2 * i : 2 * i + 2, :, cols] = v[2 * h + i].astype(BF16)
                cp.start(
                    (name, "f", h, d, part),
                    stfar.at[h, 2 * i : 2 * i + 2, :, cols],
                    w1.at[h, i, :, :, cols],
                    second(d),
                )

    def rsc_near(name, make, w1, w2, dep, part):
        cols = slice(part * cw, (part + 1) * cw)
        items = []
        for h in range(2):
            for i in range(2):
                items.append((h, pairs[1 + i][h], i if dep else 1 - i))
        v = make(items, cols)
        for h in range(2):
            _, (second, _) = axes(h)
            if dep:
                cp.arrived((name, "f", h, 1, part), (name, "f", h, -1, part))
            for i, d in enumerate((1, -1)):
                reuse(name, [("n", h, d, dep, part)])
                at = 2 * i if dep else 2 - 2 * i
                value = v[2 * h + i]
                if dep:
                    value = value + w1[h, i, :, :, cols].astype(F32)
                stnear[h, i, at : at + 2, :, cols] = value.astype(BF16)
                cp.start(
                    (name, "n", h, d, dep, part),
                    stnear.at[h, i, at : at + 2, :, cols],
                    w2.at[h, i, at : at + 2, :, cols],
                    second(d),
                )

    def rsc_own(make, part):
        cols = slice(part * cw, (part + 1) * cw)
        v = make(
            [(0, pairs[0][0], 0), (0, pairs[0][0], 1), (1, pairs[0][1], 0), (1, pairs[0][1], 1)],
            cols,
        )
        for h in range(2):
            for i in range(2):
                own[h, 2 * i : 2 * i + 2, :, cols] = v[2 * h + i]

    def rsc_second(name, w2, v1, part):
        cols = slice(part * cw, (part + 1) * cw)
        for h in range(2):
            (first, f), _ = axes(h)
            cp.arrived(*[(name, "n", h, d, dep, part) for d in (1, -1) for dep in (False, True)])
            for k in (2, 1, -1, 0):
                s = ring(f, k)
                own[h, s, :, cols] = (
                    own[h, s, :, cols]
                    + w2[h, 0, s, :, cols].astype(F32)
                    + w2[h, 1, s, :, cols].astype(F32)
                )
                if k == 2:
                    reuse(name, [("p", h, 1, part), ("p", h, -1, part)])
                    pfar[h, :, cols] = own[h, s, :, cols].astype(BF16)
                    for i, d in enumerate((1, -1)):
                        lo = 16 * i
                        cp.start(
                            (name, "p", h, d, part),
                            pfar.at[h, lo : lo + 16, cols],
                            v1.at[h, i, :, cols],
                            first(d),
                        )

    def rsc_third(name, v1, v2, part):
        cols = slice(part * cw, (part + 1) * cw)
        for h in range(2):
            (first, f), _ = axes(h)
            cp.arrived((name, "p", h, 1, part), (name, "p", h, -1, part))
            reuse(name, [("q", h, 1, part), ("q", h, -1, part)])
            for i, d in enumerate((1, -1)):
                t = ring(f, d)
                mid = slice(16 * i, 16 * i + 16)
                rest = slice(16 - 16 * i, 32 - 16 * i)
                pnear[h, i, rest, cols] = own[h, t, rest, cols].astype(BF16)
                pnear[h, i, mid, cols] = (
                    own[h, t, mid, cols] + v1[h, i, :, cols].astype(F32)
                ).astype(BF16)
                cp.start(
                    (name, "q", h, d, part), pnear.at[h, i, :, cols], v2.at[h, i, :, cols], first(d)
                )

    def rsc_last(name, v2, dst, slot, part):
        cols = slice(part * cw, (part + 1) * cw)
        for h in range(2):
            (_, f), _ = axes(h)
            cp.arrived((name, "q", h, 1, part), (name, "q", h, -1, part))
            outst[slot, h, :, cols] = (
                own[h, f, :, cols]
                + v2[h, 0, :, cols].astype(F32)
                + v2[h, 1, :, cols].astype(F32)
            ).astype(BF16)
            copy = pltpu.make_async_copy(
                outst.at[slot, h, :, cols],
                dst.at[h * half : (h + 1) * half, cols],
                out_sem.at[16 + 4 * slot + 2 * part + h],
            )
            copy.start()
            leaving.append(copy)

    def rows_of(buf, items):
        return jnp.concatenate(
            [buf[4 * h + b, c].reshape(64, buf.shape[-1]) for h, b, c in items], axis=0
        )

    def make_mixed(items, cols):
        return nn(rows_of(att, items), wo[:, cols]).reshape(4, 2, 32, cw)

    def make_gtokens(items, cols):
        v = nt(rows_of(gq, items), wq[cols, :]) + nn(rows_of(gkv, items), wkv[:, cols])
        return v.reshape(4, 2, 32, cw)

    def keys():
        return kv[:, :, :, :, 0:HEAD].reshape(1024, HEAD)

    def vals():
        return kv[:, :, :, :, HEAD : 2 * HEAD].reshape(1024, HEAD)

    def place(p):
        i, s, b, h = p & 31, (p >> 5) & 3, (p >> 7) & 3, p >> 9
        xs = jnp.where(h == 0, s, b)
        zs = jnp.where(h == 0, b, s)
        return xs * 256 + zs * 64 + h * 32 + i

    def make_mask():
        seg = segments[...].astype(F32)
        seg = jnp.concatenate([seg[n : n + 1] for n in range(8)], axis=1)
        shape = (1024, 1024)
        key_place = place(lax.broadcasted_iota(jnp.int32, (1, 1024), 1))
        pick = lax.broadcasted_iota(jnp.int32, shape, 0) == key_place
        key_seg = nn(
            jnp.broadcast_to(seg, (16, 1024)).astype(BF16), pick.astype(F32).astype(BF16)
        )[0:1]
        r = lax.broadcasted_iota(jnp.int32, (128, 1), 0)
        mine = place(((r >> 4) << 7) + core * 64 + y * 16 + (r & 15))
        here = lax.broadcasted_iota(jnp.int32, (128, 1024), 1) == mine
        my_seg = jnp.sum(jnp.where(here, seg, F32(0)), axis=1, keepdims=True)
        mask[...] = ((my_seg == key_seg) & (key_place <= mine)).astype(jnp.int32)

    def attend(part):
        def body(h, carry):
            cols = pl.ds(pl.multiple_of(h * HEAD, HEAD), HEAD)
            q = qr[:, :, cols].reshape(128, HEAD)
            s = nt(q, keys()) * scale
            s = jnp.where(mask[...] > 0, s, F32(-1e30))
            e = jnp.exp(s - jnp.max(s, axis=-1, keepdims=True))
            p = e / jnp.sum(e, axis=-1, keepdims=True)
            probs[h] = p
            o = nn(p.astype(BF16), vals()).astype(BF16)
            att[:, core, y, :, cols] = o.reshape(CHUNKS, 16, HEAD)
            return carry

        lax.fori_loop(part * heads // 4, (part + 1) * heads // 4, body, 0)

    def attend_back(part):
        if part == 0:
            dkt[...] = jnp.zeros_like(dkt)
            dvt[...] = jnp.zeros_like(dvt)

        def body(h, carry):
            cols = pl.ds(pl.multiple_of(h * HEAD, HEAD), HEAD)
            q = qr[:, :, cols].reshape(128, HEAD)
            g = gh[:, :, cols].reshape(128, HEAD)
            p = probs[h]
            dp = nt(g, vals())
            inner = jnp.sum(p * dp, axis=-1, keepdims=True)
            ds = (p * (dp - inner) * scale).astype(BF16)
            probs[h] = ds.astype(F32)
            dkt[...] += nn(q.T, ds)
            dvt[...] += nn(g.T, p.astype(BF16))
            return carry

        lax.fori_loop(part * heads // 4, (part + 1) * heads // 4, body, 0)

    def grad_query(part):
        def body(h, carry):
            cols = pl.ds(pl.multiple_of(h * HEAD, HEAD), HEAD)
            dq = nn(probs[h].astype(BF16), keys()).astype(BF16)
            gq[:, core, y, :, cols] = dq.reshape(CHUNKS, 16, HEAD)
            return carry

        lax.fori_loop(part * heads // 2, (part + 1) * heads // 2, body, 0)

    def put_dkv():
        for lo, src in ((0, dkt), (HEAD, dvt)):
            for n in range(CHUNKS):
                block = src[:, n * 128 : (n + 1) * 128].T.reshape(2, 4, 16, HEAD)
                for c in range(2):
                    pd[c, n, :, :, lo : lo + HEAD] = block[c]

    def grad_w_out(part):
        size = hn // 4
        rows = slice(part * size, (part + 1) * size)

        def body(m, carry):
            cols = pl.ds(pl.multiple_of(m * 1024, 1024), 1024)
            left = att[:, :, :, :, rows].reshape(1024, size)
            wo[rows, cols] = tn(left, grd[:, :, :, :, cols].reshape(1024, 1024)).astype(BF16)
            return carry

        lax.fori_loop(0, width // 1024, body, 0)
        copy = pltpu.make_async_copy(wo.at[rows], gwo.at[rows], out_sem.at[4 + part])
        copy.start()
        leaving.append(copy)

    def grad_w_in(part):
        size = width // 4
        rows = slice(part * size, (part + 1) * size)

        def body(m, carry):
            cols = pl.ds(pl.multiple_of(m * 512, 512), 512)
            left = tok[:, :, :, :, rows].reshape(1024, size)
            wq[rows, cols] = tn(left, gq[:, :, :, :, cols].reshape(1024, 512)).astype(BF16)
            return carry

        lax.fori_loop(0, hn // 512, body, 0)
        left = tok[:, :, :, :, rows].reshape(1024, size)
        wkv[:, rows] = tn(gkv[...].reshape(1024, 128), left).astype(BF16)
        moves = [(wq.at[rows], gwq.at[rows])]
        if part == 3:
            moves += [(wkv.at[0:64], gwk), (wkv.at[64:128], gwv)]
        for n, (src, dst) in enumerate(moves):
            copy = pltpu.make_async_copy(src, dst, out_sem.at[8 + part + n])
            copy.start()
            leaving.append(copy)

    is_low = jnp.full((128, 128), odd, jnp.int32) == 0

    def wait_local(copies):
        for copy in copies:
            copy.wait()
            leaving[:] = [c for c in leaving if c is not copy]

    def join_start():
        cp.start(("kv",), kvp, kvo, at_partner)

    def join_end():
        cp.arrived(("kv",))
        mine, other = kvp[...].reshape(128, 128), kvo[...].reshape(128, 128)
        low = jnp.where(is_low, mine, other)
        high = jnp.where(is_low, other, mine)
        joined = jnp.concatenate([low[:, :64], high[:, :64], low[:, 64:], high[:, 64:]], axis=1)
        kv[:, core, y] = joined.reshape(CHUNKS, 16, 2 * HEAD)

    def split_start():
        rs_wait("d", 0)
        for n in range(CHUNKS):
            dsum[n] = rs_value(xd, r2d, n)
        total = dsum[...].reshape(128, 2 * HEAD)
        lower = jnp.concatenate([total[:, 0:64], total[:, 128:192]], axis=1)
        upper = jnp.concatenate([total[:, 64:128], total[:, 192:256]], axis=1)
        dout[...] = jnp.where(is_low, upper, lower).astype(BF16)
        cp.start(("pair",), dout, dback, at_partner)
        dkeep[...] = jnp.where(is_low, lower, upper)

    def split_end():
        cp.arrived(("pair",))
        kept = (dkeep[...] + dback[...].astype(F32)).astype(BF16)
        gkv[:, core, y] = kept.reshape(CHUNKS, 16, 128)

    work = [
        (ag1, "t", tokens, tok),
        (start_local, loads[0:6]),
        (wait_local, own_copies[0]),
        (ag1b, "t", tok),
        (ag2, "t", tok),
        (wait_local, loads[0:6]),
        (start_local, loads[6:]),
        (project, 0),
        (rs_core, "t", pt, xt, 0, 2),
        (project_kv, 0),
        (make_mask,),
        (rs_y1, "t", pt, xt, r1t, 0, 2),
        (ag2b, "t", tok),
        (wait_local, loads[6:]),
        (ag2c, "t", tok),
        (ag2_end, "t"),
        (project_kv, 2),
        (ag1, "g", grad_out, grd),
        (project_kv, 1),
        (rs_core, "v", pv, xv, 0, 6),
        (project, 2),
        (rs_core, "t", pt, xt, 4, 2),
        (rs_y2, "t", xt, r1t, r2t, 0, 2),
        (project, 1),
        (rs_y1, "v", pv, xv, r1v, 0, 6),
        (rs_core, "t", pt, xt, 2, 2),
        (ag_end, "t"),
        (project_kv, 3),
        (rs_y1, "t", pt, xt, r1t, 4, 2),
        (send_kv,),
        (project, 3),
        (ag1b, "g", grd),
        (rs_core, "t", pt, xt, 6, 2),
        (rs_y2, "v", xv, r1v, r2v, 0, 6),
        (fin_tokens, 0, 2),
        (rs_y1, "t", pt, xt, r1t, 2, 2),
        (wait_local, own_copies[1]),
        (rs_y2, "t", xt, r1t, r2t, 4, 2),
        (rs_y1, "t", pt, xt, r1t, 6, 2),
        (fin_kv_late,),
        (ag2, "g", grd),
        (project_grad, 0),
        (fin_kv, 0, 6),
        (join_start,),
        (rs_y2, "t", xt, r1t, r2t, 2, 2),
        (rs_core, "g", pg, xg, 0, 2),
        (fin_tokens, 4, 2),
        (join_end,),
        (ag2b, "g", grd),
        (agr1, "k", kv, None),
        (rs_y1_low, "g", pg, xg, lowg, r1g, 0, 2),
        (rs_y2, "t", xt, r1t, r2t, 6, 2),
        (ag2c, "g", grd),
        (ag2_end, "g"),
        (project_grad, 1),
        (rs_core, "g", pg, xg, 2, 2),
        (fin_tokens, 2, 2),
        (agr2, "k", kv, None),
        (project_grad, 2),
        (rs_y2_low, "g", xg, lowg, r1g, r2g, 0, 2),
        (rs_core, "g", pg, xg, 4, 2),
        (rs_y1_low, "g", pg, xg, lowg, r1g, 2, 2),
        (ag_end, "g"),
        (project_grad, 3),
        (agr3, "k", kv, None),
        (rs_y1_low, "g", pg, xg, lowg, r1g, 4, 2),
        (rs_core, "g", pg, xg, 6, 2),
        (fin_grads, 0, 2),
        (fin_tokens, 6, 2),
        (rs_y2_low, "g", xg, lowg, r1g, r2g, 2, 2),
        (agr_end, "k"),
        (attend, 1),
        (rs_y2_low, "g", xg, lowg, r1g, r2g, 4, 2),
        (rs_y1_low, "g", pg, xg, lowg, r1g, 6, 2),
        (attend, 0),
        (agr1, "o0", att, 0),
        (attend, 2),
        (attend, 3),
        (rs_y2_low, "g", xg, lowg, r1g, r2g, 6, 2),
        (agr1, "o1", att, 1),
        (fin_grads, 4, 2),
        (fin_grads, 2, 2),
        (agr2, "o0", att, 0),
        (fin_grads, 6, 2),
        (attend_back, 0),
        (attend_back, 1),
        (agr2, "o1", att, 1),
        (attend_back, 2),
        (agr3, "o0", att, 0),
        (attend_back, 3),
        (put_dkv,),
        (rs_core, "d", pd, xd, 0, 8),
        (grad_query, 1),
        (agr3, "o1", att, 1),
        (agr_end, "o0"),
        (grad_query, 0),
        (rs_y1_low, "d", pd, xd, lowd, r1d, 0, 8),
        (agr_end, "o1"),
        (rsc_far, "m", make_mixed, f1.at[0], 1),
        (agr1, "q1", gq, 1),
        (agr1, "q0", gq, 0),
        (rsc_far, "m", make_mixed, f1.at[0], 0),
        (rsc_near, "m", make_mixed, f1.at[0], f2.at[0], False, 1),
        (rsc_own, make_mixed, 1),
        (rs_y2_low, "d", xd, lowd, r1d, r2d, 0, 8),
        (rsc_near, "m", make_mixed, f1.at[0], f2.at[0], False, 0),
        (rsc_own, make_mixed, 0),
        (rsc_near, "m", make_mixed, f1.at[0], f2.at[0], True, 1),
        (agr2, "q1", gq, 1),
        (rsc_near, "m", make_mixed, f1.at[0], f2.at[0], True, 0),
        (agr2, "q0", gq, 0),
        (grad_w_out, 1),
        (split_start,),
        (agr3, "q1", gq, 1),
        (grad_w_out, 0),
        (agr3, "q0", gq, 0),
        (agr_end, "q1"),
        (split_end,),
        (spread, "w", gkv),
        (grad_w_out, 2),
        (agr_end, "q0"),
        (rsc_second, "m", f2.at[0], n1.at[0], 1),
        (grad_w_out, 3),
        (rsc_second, "m", f2.at[0], n1.at[0], 0),
        (rsc_third, "m", n1.at[0], n2.at[0], 1),
        (spread_end, "w"),
        (rsc_far, "x", make_gtokens, f1.at[1], 1),
        (rsc_far, "x", make_gtokens, f1.at[1], 0),
        (rsc_third, "m", n1.at[0], n2.at[0], 0),
        (rsc_near, "x", make_gtokens, f1.at[1], f2.at[1], False, 0),
        (rsc_near, "x", make_gtokens, f1.at[1], f2.at[1], False, 1),
        (rsc_last, "m", n2.at[0], mixed, 0, 1),
        (rsc_near, "x", make_gtokens, f1.at[1], f2.at[1], True, 1),
        (rsc_near, "x", make_gtokens, f1.at[1], f2.at[1], True, 0),
        (rsc_last, "m", n2.at[0], mixed, 0, 0),
        (rsc_own, make_gtokens, 1),
        (rsc_own, make_gtokens, 0),
        (grad_w_in, 2),
        (grad_w_in, 1),
        (grad_w_in, 0),
        (rsc_second, "x", f2.at[1], n1.at[1], 1),
        (grad_w_in, 3),
        (rsc_second, "x", f2.at[1], n1.at[1], 0),
        (rsc_third, "x", n1.at[1], n2.at[1], 1),
        (rsc_third, "x", n1.at[1], n2.at[1], 0),
        (rsc_last, "x", n2.at[1], gtokens, 1, 1),
        (rsc_last, "x", n2.at[1], gtokens, 1, 0),
    ]
    for step in work[:STOP]:
        step[0](*step[1:])
    wait_local(list(leaving))
    cp.finish()


def hand_over(arrays):
    count = len(arrays)
    pieces = [max(1, a.size // 2**18) for a in arrays]
    total = sum(pieces)

    def body(*refs):
        sources, results, held = refs[:count], refs[count : 2 * count], refs[2 * count : 3 * count]
        came, went = refs[-2:]
        moves = []
        for n in range(count):
            rows = arrays[n].shape[0] // pieces[n]
            for k in range(pieces[n]):
                at, m = pl.ds(k * rows, rows), len(moves)
                moves.append(
                    (
                        pltpu.make_async_copy(sources[n].at[at], held[n].at[at], came.at[m]),
                        pltpu.make_async_copy(held[n].at[at], results[n].at[at], went.at[m]),
                    )
                )
        for come, _ in moves:
            come.start()
        for come, go in moves:
            come.wait()
            go.start()
        for _, go in moves:
            go.wait()

    anywhere = pl.BlockSpec(memory_space=pl.ANY)
    return pl.pallas_call(
        body,
        out_shape=tuple(jax.ShapeDtypeStruct(a.shape, a.dtype) for a in arrays),
        in_specs=[anywhere] * count,
        out_specs=(anywhere,) * count,
        scratch_shapes=[
            *(pltpu.VMEM(a.shape, a.dtype) for a in arrays),
            pltpu.SemaphoreType.DMA((total,)),
            pltpu.SemaphoreType.DMA((total,)),
        ],
        compiler_params=pltpu.CompilerParams(vmem_limit_bytes=VMEM_LIMIT),
    )(*arrays)


def shards(tokens, segment_ids, w_query, w_key, value_weight, w_out, grad_out):
    width = tokens.shape[1]
    hn = w_query.shape[1]
    heads = hn // HEAD
    def vm(shape, dtype=BF16):
        return pltpu.VMEM(shape, dtype)

    def rs_scratch(n):
        return [
            vm((2, CHUNKS, 4, 16, n), F32),
            vm((CHUNKS, 4, 16, n), F32),
            vm((2, CHUNKS, 8, n), F32),
            vm((2, CHUNKS, 16, n), F32),
        ]

    scratch = [
        vm((2, 4, 4, 32, width)),
        vm((2, 4, 4, 32, width)),
        vm((width, hn)),
        vm((128, width)),
        vm((hn, width)),
        *rs_scratch(hn),
        *rs_scratch(128),
        vm((7, 2, 16, 128), F32),
        vm((2, CHUNKS, 4, 16, hn), F32),
        vm((CHUNKS, 4, 16, hn), F32),
        vm((CHUNKS, 4, 16, hn)),
        vm((2, CHUNKS, 16, hn // 2)),
        vm((2, CHUNKS, 16, hn)),
        vm((2, CHUNKS, 4, 16, 2 * HEAD), F32),
        vm((CHUNKS, 4, 16, 2 * HEAD), F32),
        vm((CHUNKS, 4, 16, 2 * HEAD)),
        vm((2, CHUNKS, 16, HEAD)),
        vm((2, CHUNKS, 16, 2 * HEAD)),
        vm((CHUNKS, 16, hn)),
        vm((CHUNKS, 16, 128)),
        vm((CHUNKS, 16, 128)),
        vm((CHUNKS, 16, hn)),
        vm((CHUNKS, 2, 4, 16, 2 * HEAD)),
        vm((128, 1024), jnp.int32),
        vm((heads, 128, 1024), F32),
        vm((HEAD, 1024), F32),
        vm((HEAD, 1024), F32),
        vm((CHUNKS, 16, 2 * HEAD), F32),
        vm((128, 128)),
        vm((128, 128)),
        vm((128, 128), F32),
        vm((CHUNKS, 2, 4, 16, hn)),
        vm((CHUNKS, 2, 4, 16, hn)),
        vm((CHUNKS, 2, 4, 16, 128)),
        vm((2, 4, 32, width)),
        vm((2, 2, 4, 32, width)),
        vm((2, 4, 32, width), F32),
        vm((2, 2, 2, 2, 32, width)),
        vm((2, 2, 2, 4, 32, width)),
        vm((2, 2, 2, 16, width)),
        vm((2, 2, 2, 32, width)),
        vm((2, 32, width)),
        vm((2, 2, 32, width)),
        vm((2, 2, 32, width)),
        pltpu.SemaphoreType.DMA((SEMS,)),
        pltpu.SemaphoreType.DMA((SEMS,)),
        pltpu.SemaphoreType.DMA((16,)),
        pltpu.SemaphoreType.DMA((24,)),
    ]
    anywhere = pl.BlockSpec(memory_space=pl.ANY)
    inside = pl.BlockSpec(memory_space=pltpu.VMEM)
    shape = jax.ShapeDtypeStruct
    made = pl.pallas_call(
        kernel,
        out_shape=(
            shape((64, width), BF16),
            shape((64, width), BF16),
            shape((width, hn), BF16),
            shape((64, width), BF16),
            shape((64, width), BF16),
            shape((hn, width), BF16),
        ),
        in_specs=[anywhere] * 6 + [inside],
        out_specs=(anywhere,) * 6,
        scratch_shapes=scratch,
        compiler_params=pltpu.CompilerParams(
            collective_id=0, has_side_effects=True, vmem_limit_bytes=VMEM_LIMIT
        ),
    )(
        tokens, grad_out, w_query, w_key.T, value_weight.T, w_out, segment_ids.reshape(8, 128)
    )
    mixed, gtokens, gwq, gwk, gwv, gwo = hand_over(made)
    return mixed, gtokens, gwq, gwk.T, gwv.T, gwo


def solution(mesh):
    placed = (
        P("col", "row"),
        P(),
        P("row", "col"),
        P("row", "col"),
        P("row", "col"),
        P("col", "row"),
        P("col", "row"),
    )
    return jax.shard_map(
        shards,
        mesh=mesh,
        in_specs=placed,
        out_specs=(
            P("col", "row"),
            P("col", "row"),
            P("row", "col"),
            P("row", "col"),
            P("row", "col"),
            P("col", "row"),
        ),
        check_vma=False,
    )
```
